32 devices in a mesh: ctx: 8 (over z, y), exp: 4 (over x, core).
Axes of the slice: x: 2, y: 2, z: 4, core: 2. Of those that a mesh axis runs over, the one named last changes fastest.
Arguments:
- stream_in: bfloat16 [1024, 6144], P('ctx'), may hold values from -41 to 41
- queries: bfloat16 [1024, 8192], P('ctx', 'exp'), may hold values from -6 to 6
- key_proj: bfloat16 [1024, 8192], P('ctx', 'exp'), may hold values from -0.5390625 to 0.5390625
- values: bfloat16 [1024, 8192], P('ctx', 'exp'), may hold values from -6 to 6
- attn_gate: bfloat16 [1024, 8192], P('ctx', 'exp'), may hold values from -6 to 6
- decay_rates: float32 [64], P('exp'), may hold values from 4.8828125e-05 to 0.05
- attn_gain: float32 [8192], P('exp'), may hold values from 0.25 to 1.75
- out_weight: bfloat16 [8192, 6144], P('exp', 'ctx'), may hold values from -0.0625 to 0.0625
- ffn_gain: float32 [6144], replicated, may hold values from 0.25 to 1.75
- routing: int32 [1024, 2], P('ctx'), may hold values from 0 to 31, as said below
- route_weights: float32 [1024, 2], P('ctx'), may hold values from 0.25 to 1
- w_gate: bfloat16 [4, 6144, 9216], P('exp', None, 'ctx'), may hold values from -0.078125 to 0.078125
- w_up: bfloat16 [4, 6144, 9216], P('exp', None, 'ctx'), may hold values from -0.078125 to 0.078125
- w_down: bfloat16 [4, 9216, 6144], P('exp', 'ctx'), may hold values from -0.0625 to 0.0625
Outputs:
- residual_out: bfloat16 [1024, 6144], P(('ctx', 'exp'))
- expert_out: bfloat16 [8, 4, 8, 6144], P('ctx', 'exp')
The draws below stay inside these ranges and needn't reach their ends.
Inputs may be any that keep to these rules, and one draw needn't show every extreme that they name: `routing`: the two ids of a row differ and at most one of them is below 4. In each aligned block of 128 rows (one context shard) an id below 4 is named by at most 8 rows; one such id, the same for all blocks, is named by exactly 8 rows in every block.
All inputs are finite; a program needn't handle non-finite values.
Results may differ from the reference program's by a relative error of at most 0.025.
Values may be sent and summed in bfloat16 or wider, within the bound.
No kernel may reach another device: no remote copies, remote signals or barrier semaphores. Data moves between devices by JAX's collectives and lax.ppermute only.
A program may use at most 128 MiB of HBM per device.

```python
import math
import jax
import jax.numpy as jnp
from jax import lax

D = 6144
HEADS = 64
DH = 128
FF = 9216
ROUTED = 32
TOPK = 2
TOK = 128
SEQ = 1024
EXPERTS = 4
CAP = 8
N_CTX = 8
N_EXP = 4


def draw_stream_in(key, part):
    key_base, key_rows, key_cols = jax.random.split(key, 3)
    base_values = jnp.clip(jax.random.normal(key_base, (SEQ, D), jnp.float32), -4.0, 4.0)
    row_scale = jnp.exp(jax.random.uniform(key_rows, (SEQ, 1), jnp.float32, -1.15, 1.15))
    col_scale = jnp.exp(jax.random.uniform(key_cols, (1, D), jnp.float32, -1.15, 1.15))
    return (base_values * row_scale * col_scale).astype(jnp.bfloat16)


def draw_decay_rates(key, part):
    key_kind, key_slow, key_fast = jax.random.split(key, 3)
    slow_heads = jax.random.randint(key_kind, (HEADS,), 0, 2) > 0
    slow_rate = jnp.exp(math.log(0.05 / SEQ) + jax.random.uniform(key_slow, (HEADS,), jnp.float32) * math.log(20.0))
    fast_rate = jnp.exp(math.log(0.02) + jax.random.uniform(key_fast, (HEADS,), jnp.float32) * math.log(2.5))
    return jnp.where(slow_heads, slow_rate, fast_rate)


def draw_routing(key, part):
    key_full, key_counts, key_order, key_other, key_step, key_swap = jax.random.split(key, 6)
    full_expert = jax.random.randint(key_full, (), 0, EXPERTS)
    slot_counts = jax.random.randint(key_counts, (N_CTX, EXPERTS), 1, CAP // 2 + 1)
    slot_counts = jnp.where(jnp.arange(EXPERTS)[None, :] == full_expert, CAP, slot_counts)
    shuffle_order = jax.vmap(lambda one_key: jax.random.permutation(one_key, TOK))(jax.random.split(key_order, N_CTX))
    inverse_order = jnp.argsort(shuffle_order, axis=1, stable=True)
    slot_position = jnp.arange(TOK, dtype=jnp.int32)
    slot_owner = slot_position // CAP
    slot_within = slot_position % CAP
    owner_clipped = jnp.minimum(slot_owner, EXPERTS - 1)
    slot_limit = slot_counts[:, owner_clipped]
    slot_live = (slot_owner[None, :] < EXPERTS) & (slot_within[None, :] < slot_limit)
    held_grid = jnp.where(slot_live, slot_owner[None, :], -1)
    token_held = jnp.take_along_axis(held_grid, inverse_order, axis=1).reshape(SEQ)
    other_first = jax.random.randint(key_other, (SEQ,), EXPERTS, ROUTED)
    other_second = EXPERTS + (other_first - EXPERTS + jax.random.randint(key_step, (SEQ,), 1, ROUTED - EXPERTS)) % (ROUTED - EXPERTS)
    first_id = jnp.where(token_held >= 0, token_held, other_first)
    swap_flag = jax.random.randint(key_swap, (SEQ,), 0, 2)
    column_zero = jnp.where(swap_flag == 1, other_second, first_id)
    column_one = jnp.where(swap_flag == 1, first_id, other_second)
    return jnp.stack([column_zero, column_one], axis=1).astype(jnp.int32)


def levels(own_key, dims, cuts, least, largest):
    def one(dim, shards_of):
        steps = jax.random.uniform(jax.random.fold_in(jax.random.fold_in(own_key, 6), dim), (shards_of,), jnp.float32, least / len(cuts), largest / len(cuts))
        return jnp.repeat(jnp.exp(steps), dims[dim] // shards_of).reshape((-1,) + (1,) * (len(dims) - dim - 1))

    gain = one(*cuts[0])
    for cut in cuts[1:]:
        gain = gain * one(*cut)
    return gain


def scatter_about(stream_key, extent, width, most, shards=(), kind=jnp.bfloat16):
    array = jax.random.normal(stream_key, extent, jnp.float32) * width
    if len(shards) > 0:
        array = levels(stream_key, extent, shards, -0.22, 0.18) * array
    return jnp.clip(array, min=-most, max=most).astype(kind)


def setup_inputs(seed: int = 0) -> dict:
    streams_of = jax.random.split(jax.random.key(seed), 15)
    return {
        "stream_in": draw_stream_in(jax.random.fold_in(streams_of[14], 71), 0),
        "queries": scatter_about(streams_of[1], (SEQ, HEADS * DH), 1.0, 6.0, ((0, 8), (1, 4))),
        "key_proj": scatter_about(streams_of[2], (SEQ, HEADS * DH), 0.09, 0.5390625, ((0, 8), (1, 4))),
        "values": scatter_about(streams_of[3], (SEQ, HEADS * DH), 1.0, 6.0, ((0, 8), (1, 4))),
        "attn_gate": scatter_about(streams_of[4], (SEQ, HEADS * DH), 1.0, 6.0, ((0, 8), (1, 4))),
        "decay_rates": draw_decay_rates(jax.random.fold_in(streams_of[14], 71), 0),
        "attn_gain": jnp.clip(1.0 + 0.15 * jax.random.normal(streams_of[6], (HEADS * DH,), jnp.float32), 0.25, 1.75),
        "out_weight": scatter_about(streams_of[7], (HEADS * DH, D), (HEADS * DH) ** -0.5, 0.0625, ((0, 4), (1, 8))),
        "ffn_gain": jnp.clip(1.0 + 0.15 * jax.random.normal(streams_of[8], (D,), jnp.float32), 0.25, 1.75),
        "routing": draw_routing(jax.random.fold_in(streams_of[14], 71), 0),
        "route_weights": jnp.clip(0.25 + 0.75 * jax.random.uniform(streams_of[10], (SEQ, TOPK), jnp.float32) ** levels(streams_of[10], (SEQ, TOPK), ((0, 8),), -0.2, 0.2), 0.25, 1.0),
        "w_gate": scatter_about(streams_of[11], (EXPERTS, D, FF), D ** -0.5, 0.078125, ((0, 4), (2, 8))),
        "w_up": scatter_about(streams_of[12], (EXPERTS, D, FF), D ** -0.5, 0.078125, ((0, 4), (2, 8))),
        "w_down": scatter_about(streams_of[13], (EXPERTS, FF, D), FF ** -0.5, 0.0625, ((0, 4), (1, 8))),
    }


HIGHEST = lax.Precision.HIGHEST

def lightning(queries, key_proj, values, decay_rates):
    query_blocks = queries.reshape(N_CTX, TOK, HEADS, DH)
    key_blocks = key_proj.reshape(N_CTX, TOK, HEADS, DH)
    value_blocks = values.reshape(N_CTX, TOK, HEADS, DH)
    position = jnp.arange(TOK).astype(jnp.float32)
    distance = position[:, None] - position[None, :]
    decay_mask = jnp.where(distance[None] >= 0.0, jnp.exp(-decay_rates[:, None, None] * jnp.maximum(distance, 0.0)[None]), 0.0)
    lead_decay = jnp.exp(-decay_rates[None, :] * (position + 1.0)[:, None])
    tail_decay = jnp.exp(-decay_rates[None, :] * (TOK - 1.0 - position)[:, None])
    span_decay = jnp.exp(-decay_rates * TOK)

    def advance(carry_state, pieces):
        query_rows, key_rows, value_rows = pieces
        query_wide = query_rows.astype(jnp.float32)
        key_wide = key_rows.astype(jnp.float32)
        value_wide = value_rows.astype(jnp.float32)
        scores = jnp.einsum('ihd,jhd->hij', query_wide, key_wide)
        rounded = lax.optimization_barrier((scores * decay_mask).astype(jnp.bfloat16))
        near_part = jnp.einsum('hij,jhd->ihd', rounded.astype(jnp.float32), value_wide)
        far_part = jnp.einsum('ihd,hde->ihe', query_wide * lead_decay[:, :, None], carry_state, precision=HIGHEST)
        fresh_state = jnp.einsum('jhd,jhe->hde', key_wide * tail_decay[:, :, None], value_wide, precision=HIGHEST)
        return (span_decay[:, None, None] * carry_state + fresh_state, near_part + far_part)
    start_state = jnp.zeros((HEADS, DH, DH), jnp.float32)
    _, attended = lax.scan(advance, start_state, (query_blocks, key_blocks, value_blocks))
    return attended.reshape(N_CTX * TOK, HEADS, DH)

def reference(stream_in, queries, key_proj, values, attn_gate, decay_rates, attn_gain, out_weight, ffn_gain, routing, route_weights, w_gate, w_up, w_down):
    attended = lightning(queries, key_proj, values, decay_rates)
    inverse = lax.rsqrt(lax.optimization_barrier(jnp.mean(attended * attended, axis=2, keepdims=True)) + 1e-06)
    normed = (attended * inverse).reshape(SEQ, HEADS * DH)
    mixed_heads = (normed * attn_gain[None, :] * jax.nn.sigmoid(attn_gate.astype(jnp.float32))).astype(jnp.bfloat16)
    group_width = HEADS // N_EXP * DH
    projected = jnp.zeros((SEQ, D), jnp.float32)
    for group_index in range(N_EXP):
        part_rows = jnp.dot(mixed_heads[:, group_index * group_width:(group_index + 1) * group_width], out_weight[group_index * group_width:(group_index + 1) * group_width], preferred_element_type=jnp.float32)
        projected = projected + lax.optimization_barrier(part_rows.astype(jnp.bfloat16)).astype(jnp.float32)
    residual_out = (stream_in.astype(jnp.float32) + projected).astype(jnp.bfloat16)
    held_ids = jnp.arange(EXPERTS, dtype=jnp.int32)
    route_blocks = routing.reshape(N_CTX, TOK, TOPK)
    hit_mask = route_blocks[..., None] == held_ids
    member = lax.optimization_barrier(jnp.sum(hit_mask.astype(jnp.int32), axis=2)).astype(jnp.int32)
    slot_rank = (jnp.cumsum(member, axis=1) - 1).astype(jnp.int32)
    pick_mask = (member[..., None] == 1) & (slot_rank[..., None] == jnp.arange(CAP, dtype=jnp.int32))
    gate_of = lax.optimization_barrier(jnp.sum(jnp.where(hit_mask, route_weights.reshape(N_CTX, TOK, TOPK)[..., None], 0.0), axis=2))
    slot_weight = lax.optimization_barrier(jnp.sum(jnp.where(pick_mask, gate_of[..., None], 0.0), axis=1))
    slot_hidden = jnp.einsum('ctes,ctd->cesd', pick_mask.astype(jnp.float32), residual_out.reshape(N_CTX, TOK, D).astype(jnp.float32))
    slot_scale = lax.rsqrt(lax.optimization_barrier(jnp.mean(slot_hidden * slot_hidden, axis=3, keepdims=True)) + 1e-06)
    slot_inputs = (slot_hidden * slot_scale * ffn_gain).astype(jnp.bfloat16)
    group_hidden = FF // N_CTX
    outputs = []
    for expert_index in range(EXPERTS):
        expert_rows = slot_inputs[:, expert_index].reshape(N_CTX * CAP, D)
        gate_part = jnp.dot(expert_rows, w_gate[expert_index], preferred_element_type=jnp.float32)
        up_part = jnp.dot(expert_rows, w_up[expert_index], preferred_element_type=jnp.float32)
        activated = (jax.nn.silu(gate_part) * up_part).astype(jnp.bfloat16)
        act_groups = activated.reshape(N_CTX * CAP, N_CTX, group_hidden).transpose(1, 0, 2)
        down_groups = w_down[expert_index].reshape(N_CTX, group_hidden, D)

        def accumulate(running, pieces):
            act_rows, down_rows = pieces
            part_rows = jnp.dot(act_rows, down_rows, preferred_element_type=jnp.float32)
            return (running + lax.optimization_barrier(part_rows.astype(jnp.bfloat16)).astype(jnp.float32), None)
        summed_down, _ = lax.scan(accumulate, jnp.zeros((N_CTX * CAP, D), jnp.float32), (act_groups, down_groups))
        outputs.append(summed_down.reshape(N_CTX, CAP, D))
    totals = jnp.stack(outputs, axis=1)
    expert_out = (totals * slot_weight[..., None]).astype(jnp.bfloat16)
    return (residual_out, expert_out)
```

```python
import functools

import jax
import jax.numpy as jnp
from jax import lax
from jax.experimental import pallas as pl
from jax.experimental.pallas import tpu as pltpu
from jax.sharding import PartitionSpec as P

CHUNKS = 2
F32 = jnp.float32
BF16 = jnp.bfloat16
VMEM = pl.BlockSpec(memory_space=pltpu.VMEM)
SMEM = pl.BlockSpec(memory_space=pltpu.SMEM)


def rows_iota(shape):
    return lax.broadcasted_iota(jnp.int32, shape, 0).astype(F32)


def cols_iota(shape):
    return lax.broadcasted_iota(jnp.int32, shape, 1).astype(F32)


def lanes(head, size):
    return pl.ds(pl.multiple_of(head * size, size), size)


def state_kernel(per_half, place_ref, decay_ref, k_ref, v_ref, *outs):
    pair = place_ref[0]
    tok, size = k_ref.shape[0], outs[0].shape[1]
    back = (tok - 1.0) - rows_iota((tok, size))
    for chunk in range(CHUNKS):
        for which in range(2):
            out = outs[chunk * 2 + which]
            half = pair if which == 0 else 1 - pair
            for l in range(per_half):
                head = chunk * 2 * per_half + half * per_half + l
                k = k_ref[:, lanes(head, size)].astype(F32)
                k = (k * jnp.exp(-decay_ref[head] * back)).astype(BF16)
                state = lax.dot_general(
                    k,
                    v_ref[:, lanes(head, size)],
                    (((0,), (0,)), ((), ())),
                    preferred_element_type=F32,
                )
                out[l * size : (l + 1) * size, :] = state.astype(BF16)


def near_kernel(heads, decay_ref, q_ref, k_ref, v_ref, near_ref):
    tok = q_ref.shape[0]
    size = q_ref.shape[1] // heads
    gap = rows_iota((tok, tok)) - cols_iota((tok, tok))
    for head in range(heads):
        at = slice(head * size, (head + 1) * size)
        scores = lax.dot_general(
            q_ref[:, at], k_ref[:, at], (((1,), (1,)), ((), ())), preferred_element_type=F32
        )
        mask = jnp.where(gap >= 0.0, jnp.exp(-decay_ref[head] * jnp.maximum(gap, 0.0)), 0.0)
        weights = (scores * mask).astype(BF16)
        near_ref[:, at] = jnp.dot(weights, v_ref[:, at], preferred_element_type=F32)


def mix_kernel(
    chunk, per_half, own_rows, place_ref, decay_ref, q_ref, near_ref, gate_ref, gain_ref, mine_ref, other_ref, out_ref
):
    pair, own = place_ref[0], place_ref[1]
    size = mine_ref.shape[1]
    tok = q_ref.shape[0]
    ahead = rows_iota((tok, size)) + 1.0
    for which in range(2):
        prior = mine_ref if which == 0 else other_ref
        half = pair if which == 0 else 1 - pair
        for l in range(per_half):
            local = half * per_half + l
            head = chunk * 2 * per_half + local
            at = lanes(head, size)
            far = jnp.dot(
                q_ref[:, at], prior[l * size : (l + 1) * size, :], preferred_element_type=F32
            )
            attended = near_ref[:, at] + far * jnp.exp(-decay_ref[head] * ahead)
            inverse = lax.rsqrt(jnp.mean(attended * attended, axis=1, keepdims=True) + 1e-06)
            gate = jax.nn.sigmoid(gate_ref[:, at].astype(F32))
            mixed = (attended * inverse * gain_ref[:, at] * gate).astype(BF16)
            for block in range(tok // own_rows):
                to = pl.multiple_of((block ^ own) * own_rows, own_rows)
                out_ref[pl.ds(to, own_rows), lanes(local, size)] = mixed[
                    block * own_rows : (block + 1) * own_rows
                ]


def per_device(
    stream_in,
    queries,
    key_proj,
    values,
    attn_gate,
    decay_rates,
    attn_gain,
    out_weight,
    ffn_gain,
    routing,
    route_weights,
    w_gate,
    w_up,
    w_down,
):
    tok, width = stream_in.shape
    heads = decay_rates.shape[0]
    size = queries.shape[1] // heads
    n_exp, n_ctx = lax.axis_size("exp"), lax.axis_size("ctx")
    own, place = lax.axis_index("exp"), lax.axis_index("ctx")
    groups = n_ctx // 2
    group, pair = place // 2, place % 2
    cap = tok // 16
    own_rows = tok // n_exp
    cols = out_weight.shape[1]
    per_half = heads // (2 * CHUNKS)
    swap = [(i, i ^ 1) for i in range(n_ctx)]
    line = [(i, i + 2) for i in range(n_ctx - 2)]
    ring = [(i, (i + 2) % n_ctx) for i in range(n_ctx)]
    here = jnp.stack([pair, own]).astype(jnp.int32)

    hit = routing[:, :, None] == jnp.arange(n_exp, dtype=jnp.int32)
    member = jnp.any(hit, axis=1)
    gate_of = jnp.sum(jnp.where(hit, route_weights[:, :, None], 0.0), axis=1)
    position = jnp.arange(tok, dtype=jnp.int32)
    before = (position[:, None] > position[None, :]).astype(BF16)
    rank = jnp.dot(before, member.astype(BF16), preferred_element_type=F32)
    pick = member[:, :, None] & (rank[:, :, None] == jnp.arange(cap, dtype=F32))
    number = jnp.sum(jnp.where(pick, (position + 1).astype(F32)[:, None, None], 0.0), axis=0)
    own_pick = lax.dynamic_index_in_dim(pick, own, 1, keepdims=False)
    own_weight = jnp.sum(
        jnp.where(own_pick, lax.dynamic_index_in_dim(gate_of, own, 1), 0.0), axis=0
    )
    stream_slots = lax.dot_general(
        own_pick.astype(BF16), stream_in, (((0,), (0,)), ((), ())), preferred_element_type=F32
    ).astype(BF16)

    states = pl.pallas_call(
        functools.partial(state_kernel, per_half),
        out_shape=[jax.ShapeDtypeStruct((per_half * size, size), BF16)] * (2 * CHUNKS),
        in_specs=[SMEM, SMEM, VMEM, VMEM],
        out_specs=[VMEM] * (2 * CHUNKS),
        name="shard_state",
    )(here, decay_rates, key_proj, values)
    near = pl.pallas_call(
        functools.partial(near_kernel, heads),
        out_shape=jax.ShapeDtypeStruct((tok, heads * size), F32),
        in_specs=[SMEM, VMEM, VMEM, VMEM],
        out_specs=VMEM,
        name="near_part",
    )(decay_rates, queries, key_proj, values)

    mixed = []
    for chunk in range(CHUNKS):
        keep, send = states[2 * chunk], states[2 * chunk + 1]
        first = chunk * 2 * per_half + pair * per_half
        rate = lax.dynamic_slice_in_dim(decay_rates, first, per_half, 0)
        rate = jnp.repeat(rate, size)[:, None]
        got = lax.ppermute(send, "ctx", swap)
        lower = jnp.where(pair == 0, keep, got).astype(F32)
        upper = jnp.where(pair == 0, got, keep).astype(F32)
        span = jnp.exp(-rate * tok)
        passing = (span * lower + upper).astype(BF16)
        prior = jnp.zeros(passing.shape, F32)
        for step in range(groups - 1):
            passing = lax.ppermute(passing, "ctx", line)
            prior = prior + jnp.exp(-rate * (2 * tok * step)) * passing.astype(F32)
        after = span * prior + lower
        mine = jnp.where(pair == 0, prior, after).astype(BF16)
        theirs = jnp.where(pair == 0, after, prior).astype(BF16)
        other = lax.ppermute(theirs, "ctx", swap)
        mixed.append(
            pl.pallas_call(
                functools.partial(mix_kernel, chunk, per_half, own_rows),
                out_shape=jax.ShapeDtypeStruct((tok, 2 * per_half * size), BF16),
                in_specs=[SMEM, SMEM, VMEM, VMEM, VMEM, VMEM, VMEM, VMEM],
                out_specs=VMEM,
                name="mix_heads",
            )(here, decay_rates, queries, near, attn_gate, attn_gain[None, :], mine, other)
        )

    parcel = stream_slots.reshape(cap, n_ctx, cols).transpose(1, 0, 2)
    label = jnp.pad(number.reshape(1, n_exp * cap), ((0, cap - 1), (0, cols - n_exp * cap)))
    label = jnp.broadcast_to(label.astype(BF16)[None], (n_ctx, cap, cols))
    arrived = lax.all_to_all(
        jnp.concatenate([parcel, label], axis=1), "ctx", split_axis=0, concat_axis=0, tiled=True
    )
    stream_rows = arrived[:, :cap].reshape(n_ctx * cap, cols)
    token = arrived[:, cap, : n_exp * cap].astype(jnp.int32).reshape(n_ctx, n_exp, cap) - 1
    shard = jnp.arange(n_ctx, dtype=jnp.int32)
    block = ((group - shard // 2) % groups) * 2 + (pair ^ (shard % 2))
    token = jnp.stack(
        [lax.dynamic_index_in_dim(token, own ^ j, 1, keepdims=False) for j in range(n_exp)]
    )
    column = block[None, :, None] * tok + ((token // own_rows) ^ own) * own_rows + token % own_rows
    column = jnp.where(token >= 0, column, -1).reshape(-1)
    chosen = (column[:, None] == jnp.arange(n_ctx * tok, dtype=jnp.int32)[None, :]).astype(BF16)

    wide = 2 * per_half * size
    totals = [None] * n_ctx
    for chunk in range(CHUNKS):
        weight = out_weight[chunk * wide : (chunk + 1) * wide]
        current = mixed[chunk]
        for step in range(groups):
            for y, rows in enumerate((current, lax.ppermute(current, "ctx", swap))):
                at = 2 * step + y
                part = jnp.dot(rows, weight, preferred_element_type=F32)
                totals[at] = part if totals[at] is None else totals[at] + part
            if step + 1 < groups:
                current = lax.ppermute(current, "ctx", ring)
    partial = jnp.concatenate([t.astype(BF16) for t in totals], axis=0)

    def add_groups(parts):
        bit = 1
        parts = list(parts)
        while bit < n_exp:
            far = [j for j in range(0, n_exp, bit) if j & bit]
            sent = jnp.stack([parts[j // bit] for j in far])
            got = lax.ppermute(sent, "exp", [(i, i ^ bit) for i in range(n_exp)])
            parts = [
                parts[j // bit - 1].astype(F32) + got[n].astype(F32) for n, j in enumerate(far)
            ]
            bit *= 2
            if bit < n_exp:
                parts = [p.astype(BF16) for p in parts]
        return parts[0]

    slot_rows = jnp.dot(chosen, partial, preferred_element_type=F32).astype(BF16)
    slot_total = add_groups(slot_rows.reshape(n_exp, n_ctx * cap, cols))
    hidden = (slot_total + stream_rows.astype(F32)).astype(BF16)

    def absolute(blocks):
        stacked = jnp.stack(blocks)
        return jnp.take(stacked, block, axis=0)

    pieces = []
    current = hidden
    for step in range(groups):
        pieces += [current, lax.ppermute(current, "ctx", swap)]
        if step + 1 < groups:
            current = lax.ppermute(current, "ctx", ring)
    slot_hidden = absolute(pieces).transpose(1, 0, 2).reshape(n_ctx * cap, width).astype(F32)
    inverse = lax.rsqrt(jnp.mean(slot_hidden * slot_hidden, axis=1, keepdims=True) + 1e-06)
    slot_inputs = (slot_hidden * inverse * ffn_gain[None, :]).astype(BF16)

    gate_part = jnp.dot(slot_inputs, w_gate[0], preferred_element_type=F32)
    up_part = jnp.dot(slot_inputs, w_up[0], preferred_element_type=F32)
    activated = (jax.nn.silu(gate_part) * up_part).astype(BF16)
    down = jnp.dot(activated, w_down[0], preferred_element_type=F32).astype(BF16)
    parts = lax.all_to_all(
        down.reshape(n_ctx, cap, width), "ctx", split_axis=0, concat_axis=0, tiled=True
    )
    summed = jnp.sum(parts.astype(F32), axis=0)
    expert_out = (summed * own_weight[:, None]).astype(BF16).reshape(1, 1, cap, width)

    bulk = partial.reshape(n_ctx, n_exp, own_rows, cols)
    bulk = add_groups([bulk[:, j] for j in range(n_exp)]).astype(BF16)
    back = []
    for step in range(groups):
        for y in range(2):
            piece = bulk[2 * step + y]
            if step or y:
                to = [(i, ((i // 2 - step) % groups) * 2 + ((i % 2) ^ y)) for i in range(n_ctx)]
                piece = lax.ppermute(piece, "ctx", to)
            back.append(piece)
    order = ((shard // 2 - group) % groups) * 2 + (pair ^ (shard % 2))
    projected = jnp.take(jnp.stack(back), order, axis=0).transpose(1, 0, 2).reshape(own_rows, width)
    stream_own = lax.dynamic_slice_in_dim(stream_in, own * own_rows, own_rows, 0)
    residual_out = (stream_own.astype(F32) + projected.astype(F32)).astype(BF16)
    return (residual_out, expert_out)


def solution(mesh):
    return jax.shard_map(
        per_device,
        mesh=mesh,
        in_specs=(
            P("ctx", None),
            P("ctx", "exp"),
            P("ctx", "exp"),
            P("ctx", "exp"),
            P("ctx", "exp"),
            P("exp"),
            P("exp"),
            P("exp", "ctx"),
            P(),
            P("ctx", None),
            P("ctx", None),
            P("exp", None, "ctx"),
            P("exp", None, "ctx"),
            P("exp", "ctx", None),
        ),
        out_specs=(P(("ctx", "exp"), None), P("ctx", "exp", None, None)),
        check_vma=False,
    )
```

```python
import functools

import jax
import jax.numpy as jnp
from jax import lax
from jax.experimental import pallas as pl
from jax.experimental.pallas import tpu as pltpu
from jax.sharding import PartitionSpec as P

CHUNKS = 2
F32 = jnp.float32
BF16 = jnp.bfloat16
VMEM = pl.BlockSpec(memory_space=pltpu.VMEM)
SMEM = pl.BlockSpec(memory_space=pltpu.SMEM)
HBM = pl.BlockSpec(memory_space=pltpu.HBM)


def limit(mib):
    return pltpu.CompilerParams(vmem_limit_bytes=mib * 2**20)


def rows_iota(shape):
    return lax.broadcasted_iota(jnp.int32, shape, 0).astype(F32)


def cols_iota(shape):
    return lax.broadcasted_iota(jnp.int32, shape, 1).astype(F32)


def lanes(head, size):
    return pl.ds(pl.multiple_of(head * size, size), size)


def after(value, *others):
    return lax.optimization_barrier((value, *others))[0]


def state_kernel(per_half, place_ref, decay_ref, k_ref, v_ref, *outs):
    pair = place_ref[0]
    tok, size = k_ref.shape[0], outs[0].shape[2]
    back = (tok - 1.0) - rows_iota((tok, size))
    for chunk in range(CHUNKS):
        for which in (1, 0):
            half = pair if which == 0 else 1 - pair
            heads = [chunk * 2 * per_half + half * per_half + l for l in range(per_half)]
            keys = [
                (k_ref[:, lanes(h, size)].astype(F32) * jnp.exp(-decay_ref[h] * back)).astype(BF16)
                for h in heads
            ]
            states = [
                lax.dot_general(
                    k,
                    v_ref[:, lanes(h, size)],
                    (((0,), (0,)), ((), ())),
                    preferred_element_type=F32,
                )
                for k, h in zip(keys, heads)
            ]
            for l, state in enumerate(states):
                outs[chunk * 2 + which][l] = state.astype(BF16)


def near_kernel(chunk, heads, decay_ref, q_ref, k_ref, v_ref, gate_ref, gain_ref, near_ref, scale_ref, query_ref):
    tok = q_ref.shape[0]
    size = near_ref.shape[1] // heads
    gap = rows_iota((tok, tok)) - cols_iota((tok, tok))
    ahead = jnp.maximum(gap, 0.0)
    for first in range(0, heads, 4):
        local = range(first, min(first + 4, heads))
        at = [slice((chunk * heads + l) * size, (chunk * heads + l + 1) * size) for l in local]
        scores = [
            lax.dot_general(
                q_ref[:, s], k_ref[:, s], (((1,), (1,)), ((), ())), preferred_element_type=F32
            )
            for s in at
        ]
        weights = []
        for l, score in zip(local, scores):
            mask = jnp.where(gap >= 0.0, jnp.exp(-decay_ref[chunk * heads + l] * ahead), 0.0)
            weights.append((score * mask).astype(BF16))
        for l, s, w in zip(local, at, weights):
            near_ref[:, l * size : (l + 1) * size] = jnp.dot(
                w, v_ref[:, s], preferred_element_type=F32
            )
    own = slice(chunk * heads * size, (chunk + 1) * heads * size)
    gate = gate_ref[:, own].astype(F32)
    scale_ref[...] = gain_ref[:, own] / (1.0 + jnp.exp(-gate))
    query_ref[...] = q_ref[:, own]


def mix_kernel(
    chunk, per_half, own_rows, place_ref, decay_ref, q_ref, near_ref, scale_ref, mine_ref, other_ref, out_ref
):
    pair, own = place_ref[0], place_ref[1]
    size = mine_ref.shape[2]
    tok = q_ref.shape[0]
    ahead = rows_iota((tok, size)) + 1.0
    for which in range(2):
        prior = mine_ref if which == 0 else other_ref
        half = pair if which == 0 else 1 - pair
        local = [half * per_half + l for l in range(per_half)]
        far = [
            jnp.dot(q_ref[:, lanes(h, size)], prior[l], preferred_element_type=F32)
            for l, h in enumerate(local)
        ]
        mixed = []
        for h, part in zip(local, far):
            decay = decay_ref[chunk * 2 * per_half + h]
            attended = near_ref[:, lanes(h, size)] + part * jnp.exp(-decay * ahead)
            inverse = lax.rsqrt(jnp.mean(attended * attended, axis=1, keepdims=True) + 1e-06)
            mixed.append((attended * inverse * scale_ref[:, lanes(h, size)]).astype(BF16))
        for h, rows in zip(local, mixed):
            for block in range(tok // own_rows):
                to = pl.multiple_of((block ^ own) * own_rows, own_rows)
                out_ref[pl.ds(to, own_rows), lanes(h, size)] = rows[
                    block * own_rows : (block + 1) * own_rows
                ]


def stage_kernel(first, w_ref, out_ref):
    pltpu.sync_copy(w_ref.at[0, pl.ds(first, out_ref.shape[0]), :], out_ref)


def ffn_kernel(n, parts, blocks, order_ref, *refs):
    pieces, refs = refs[:n], refs[n:]
    gain_ref, refs = refs[0], refs[1:]
    gates, ups, refs = refs[:parts], refs[parts : 2 * parts], refs[2 * parts :]
    down_ref, out_ref, rows_ref, down_buf, sems = refs
    step = out_ref.shape[1] // blocks
    copies = [
        pltpu.make_async_copy(
            down_ref.at[0, :, pl.ds(i * step, step)], down_buf.at[i], sems.at[i]
        )
        for i in range(blocks)
    ]
    for copy in copies:
        copy.start()
    cols = pieces[0].shape[1]
    total = 0.0
    for piece in pieces:
        wide = piece[...].astype(F32)
        total = total + jnp.sum(wide * wide, axis=1, keepdims=True)
    inverse = lax.rsqrt(total * (1.0 / (n * cols)) + 1e-06)
    for i, piece in enumerate(pieces):
        at = lanes(order_ref[i], cols) if n > 1 else slice(None)
        rows_ref[:, at] = (piece[...].astype(F32) * inverse * gain_ref[:, at]).astype(BF16)
    gate = up = None
    span = gates[0].shape[0]
    for i in range(parts):
        for j in range(0, span, span // 4):
            rows = rows_ref[:, i * span + j : i * span + j + span // 4]
            g = jnp.dot(rows, gates[i][j : j + span // 4, :], preferred_element_type=F32)
            u = jnp.dot(rows, ups[i][j : j + span // 4, :], preferred_element_type=F32)
            gate = g if gate is None else gate + g
            up = u if up is None else up + u
    activated = (gate / (1.0 + jnp.exp(-gate)) * up).astype(BF16)
    for i, copy in enumerate(copies):
        copy.wait()
        out_ref[:, i * step : (i + 1) * step] = jnp.dot(
            activated, down_buf[i], preferred_element_type=F32
        ).astype(BF16)


def per_device(
    stream_in,
    queries,
    key_proj,
    values,
    attn_gate,
    decay_rates,
    attn_gain,
    out_weight,
    ffn_gain,
    routing,
    route_weights,
    w_gate,
    w_up,
    w_down,
):
    tok, width = stream_in.shape
    heads = decay_rates.shape[0]
    size = queries.shape[1] // heads
    n_exp, n_ctx = lax.axis_size("exp"), lax.axis_size("ctx")
    own, place = lax.axis_index("exp"), lax.axis_index("ctx")
    groups = n_ctx // 2
    group, pair = place // 2, place % 2
    cap = tok // 16
    own_rows = tok // n_exp
    cols = out_weight.shape[1]
    hidden_units = w_gate.shape[2]
    per_half = heads // (2 * CHUNKS)
    per_chunk = heads // CHUNKS
    wide = per_chunk * size
    swap = [(i, i ^ 1) for i in range(n_ctx)]
    here = jnp.stack([pair, own]).astype(jnp.int32)

    def swapped(value):
        return lax.ppermute(value, "ctx", swap)

    def shifted(value, by):
        to = [(i, (i + 2 * by) % n_ctx) for i in range(n_ctx)]
        return lax.ppermute(value, "ctx", to)

    states = pl.pallas_call(
        functools.partial(state_kernel, per_half),
        out_shape=[jax.ShapeDtypeStruct((per_half, size, size), BF16)] * (2 * CHUNKS),
        in_specs=[SMEM, SMEM, VMEM, VMEM],
        out_specs=[VMEM] * (2 * CHUNKS),
        compiler_params=limit(8),
        name="shard_state",
    )(here, decay_rates, key_proj, values)

    def near_part(chunk, start):
        return pl.pallas_call(
            functools.partial(near_kernel, chunk, per_chunk),
            out_shape=[
                jax.ShapeDtypeStruct((tok, wide), F32),
                jax.ShapeDtypeStruct((tok, wide), F32),
                jax.ShapeDtypeStruct((tok, wide), BF16),
            ],
            in_specs=[SMEM] + [VMEM] * 5,
            out_specs=[VMEM] * 3,
            compiler_params=limit(8),
            name="near_part",
        )(after(decay_rates, start), queries, key_proj, values, attn_gate, attn_gain[None, :])

    rates, lowers, spans, windows, priors, nears = [], [], [], [], [], []
    for chunk in range(CHUNKS):
        keep, send = states[2 * chunk], states[2 * chunk + 1]
        got = swapped(send)
        nears.append(near_part(chunk, states[0] if chunk == 0 else windows[0]))
        first = chunk * per_chunk + pair * per_half
        rate = lax.dynamic_slice_in_dim(decay_rates, first, per_half, 0)[:, None, None]
        span = jnp.exp(-rate * tok)
        lower = jnp.where(pair == 0, keep, got).astype(F32)
        upper = jnp.where(pair == 0, got, keep).astype(F32)
        windows.append((span * lower + upper).astype(BF16))
        rates.append(rate)
        spans.append(span)
        lowers.append(lower)
        priors.append(jnp.zeros(lower.shape, F32))
    reach = 1
    while reach < groups:
        line = [(i, i + 2 * reach) for i in range(n_ctx - 2 * reach)]
        for chunk in range(CHUNKS):
            got = lax.ppermute(windows[chunk], "ctx", line).astype(F32)
            factor = jnp.exp(-rates[chunk] * (2 * tok * (reach - 1)))
            priors[chunk] = priors[chunk] + factor * got
            if 2 * reach < groups:
                factor = jnp.exp(-rates[chunk] * (2 * tok * reach))
                windows[chunk] = (windows[chunk].astype(F32) + factor * got).astype(BF16)
        reach *= 2
    mixed = []
    for chunk in range(CHUNKS):
        prior = priors[chunk]
        second = spans[chunk] * prior + lowers[chunk]
        mine = jnp.where(pair == 0, prior, second).astype(BF16)
        other = swapped(jnp.where(pair == 0, second, prior).astype(BF16))
        near, scale, query = nears[chunk]
        mixed.append(
            pl.pallas_call(
                functools.partial(mix_kernel, chunk, per_half, own_rows),
                out_shape=jax.ShapeDtypeStruct((tok, wide), BF16),
                in_specs=[SMEM, SMEM] + [VMEM] * 5,
                out_specs=VMEM,
                compiler_params=limit(8),
                name="mix_heads",
            )(here, decay_rates, query, near, scale, mine, other)
        )

    routing = after(routing, mixed[0])
    hit = routing[:, :, None] == jnp.arange(n_exp, dtype=jnp.int32)
    member = jnp.any(hit, axis=1)
    gate_of = jnp.sum(jnp.where(hit, route_weights[:, :, None], 0.0), axis=1)
    position = jnp.arange(tok, dtype=jnp.int32)
    before = (position[:, None] > position[None, :]).astype(BF16)
    rank = jnp.dot(before, member.astype(BF16), preferred_element_type=F32)
    pick = member[:, :, None] & (rank[:, :, None] == jnp.arange(cap, dtype=F32))
    number = jnp.sum(jnp.where(pick, (position + 1).astype(F32)[:, None, None], 0.0), axis=0)
    own_pick = lax.dynamic_index_in_dim(pick, own, 1, keepdims=False)
    own_weight = jnp.sum(
        jnp.where(own_pick, lax.dynamic_index_in_dim(gate_of, own, 1), 0.0), axis=0
    )
    stream_slots = lax.dot_general(
        own_pick.astype(BF16), stream_in, (((0,), (0,)), ((), ())), preferred_element_type=F32
    ).astype(BF16)
    parcel = stream_slots.reshape(cap, n_ctx, cols).transpose(1, 0, 2)
    label = jnp.pad(number.reshape(1, n_exp * cap), ((0, cap - 1), (0, cols - n_exp * cap)))
    label = jnp.broadcast_to(label.astype(BF16)[None], (n_ctx, cap, cols))
    parcel = jnp.concatenate([parcel, label], axis=1)

    totals = [None] * n_ctx
    arrived = None
    staged = {}
    parts = 2
    for chunk in range(CHUNKS):
        weight = out_weight[chunk * wide : (chunk + 1) * wide]
        current, crossed = mixed[chunk], None
        for step in range(groups):
            if chunk % 2 and step == 1:
                crossed = shifted(crossed, 1)
            else:
                crossed = swapped(current)
            for y, rows in enumerate((current, crossed)):
                at = 2 * step + y
                part = jnp.dot(rows, weight, preferred_element_type=F32)
                totals[at] = part if totals[at] is None else totals[at] + part
            if step + 1 < groups:
                current = shifted(current, 1)
            if chunk == CHUNKS - 1 and step < parts:
                for name, w in (("gate", w_gate), ("up", w_up)):
                    staged[name, step] = pl.pallas_call(
                        functools.partial(stage_kernel, step * (width // parts)),
                        out_shape=pltpu.VMEM((width // parts, hidden_units), BF16),
                        in_specs=[HBM],
                        out_specs=VMEM,
                        compiler_params=limit(2),
                        name="stage_weight",
                    )(pltpu.with_memory_space_constraint(after(w, current), pltpu.HBM))
        if chunk == 0:
            arrived = lax.all_to_all(
                after(parcel, current), "ctx", split_axis=0, concat_axis=0, tiled=True
            )
    partial = jnp.concatenate([t.astype(BF16) for t in totals], axis=0)

    stream_rows = arrived[:, :cap].reshape(n_ctx * cap, cols)
    token = arrived[:, cap, : n_exp * cap].astype(jnp.int32).reshape(n_ctx, n_exp, cap) - 1
    shard = jnp.arange(n_ctx, dtype=jnp.int32)
    block = ((group - shard // 2) % groups) * 2 + (pair ^ (shard % 2))
    token = jnp.stack(
        [lax.dynamic_index_in_dim(token, own ^ j, 1, keepdims=False) for j in range(n_exp)]
    )
    column = block[None, :, None] * tok + ((token // own_rows) ^ own) * own_rows + token % own_rows
    column = jnp.where(token >= 0, column, -1).reshape(-1)
    chosen = (column[:, None] == jnp.arange(n_ctx * tok, dtype=jnp.int32)[None, :]).astype(BF16)

    def add_groups(parts):
        bit = 1
        parts = list(parts)
        while bit < n_exp:
            far = [j for j in range(0, n_exp, bit) if j & bit]
            sent = jnp.stack([parts[j // bit] for j in far])
            got = lax.ppermute(sent, "exp", [(i, i ^ bit) for i in range(n_exp)])
            parts = [
                parts[j // bit - 1].astype(F32) + got[n].astype(F32) for n, j in enumerate(far)
            ]
            bit *= 2
            if bit < n_exp:
                parts = [p.astype(BF16) for p in parts]
        return parts[0]

    slot_rows = jnp.dot(chosen, partial, preferred_element_type=F32).astype(BF16)
    slot_total = add_groups(slot_rows.reshape(n_exp, n_ctx * cap, cols))
    hidden = (slot_total + stream_rows.astype(F32)).astype(BF16)

    pieces = {0: hidden}
    bit = 1
    while bit < groups:
        for r in range(bit):
            pieces[r | bit] = lax.ppermute(
                pieces[r], "ctx", [(i, i ^ (2 * bit)) for i in range(n_ctx)]
            )
        bit *= 2
    pieces = [p for r in range(groups) for p in (pieces[r], swapped(pieces[r]))]
    source = (place ^ shard).astype(jnp.int32)
    if cols % 128:
        pieces = [jnp.take(jnp.stack(pieces), source, axis=0).transpose(1, 0, 2).reshape(-1, width)]
    blocks = 8
    down = pl.pallas_call(
        functools.partial(ffn_kernel, len(pieces), parts, blocks),
        out_shape=jax.ShapeDtypeStruct((n_ctx * cap, width), BF16),
        in_specs=[SMEM] + [VMEM] * (len(pieces) + 1 + 2 * parts) + [HBM],
        out_specs=VMEM,
        scratch_shapes=[
            pltpu.VMEM((n_ctx * cap, width), BF16),
            pltpu.VMEM((blocks, hidden_units, width // blocks), BF16),
            pltpu.SemaphoreType.DMA((blocks,)),
        ],
        compiler_params=limit(24),
        name="expert",
    )(
        source,
        *pieces,
        ffn_gain[None, :],
        *(
            pltpu.with_memory_space_constraint(staged[name, i], pltpu.VMEM)
            for name in ("gate", "up")
            for i in range(parts)
        ),
        pltpu.with_memory_space_constraint(w_down, pltpu.HBM),
    )
    received = lax.all_to_all(
        down.reshape(n_ctx, cap, width), "ctx", split_axis=0, concat_axis=0, tiled=True
    )
    summed = jnp.sum(received.astype(F32), axis=0)
    expert_out = (summed * own_weight[:, None]).astype(BF16).reshape(1, 1, cap, width)

    bulk = after(partial, hidden).reshape(groups, 2, n_exp, own_rows, cols)
    bulk = add_groups([bulk[:, :, j] for j in range(n_exp)]).astype(BF16)
    bulk = [bulk[:, 0], swapped(bulk[:, 1])]
    bulk = [jnp.stack([bulk[0][k], bulk[1][k]]) for k in range(groups)]
    bit = 1
    while bit < groups:
        moving = [k for k in range(groups) if k & bit]
        moved = shifted(jnp.stack([bulk[k] for k in moving]), -bit)
        for n, k in enumerate(moving):
            bulk[k] = moved[n]
        bit *= 2
    order = ((shard // 2 - group) % groups) * 2 + (pair ^ (shard % 2))
    projected = jnp.take(jnp.concatenate(bulk), order, axis=0).transpose(1, 0, 2)
    projected = projected.reshape(own_rows, width)
    stream_own = lax.dynamic_slice_in_dim(stream_in, own * own_rows, own_rows, 0)
    residual_out = (stream_own.astype(F32) + projected.astype(F32)).astype(BF16)
    return (residual_out, expert_out)


def solution(mesh):
    return jax.shard_map(
        per_device,
        mesh=mesh,
        in_specs=(
            P("ctx", None),
            P("ctx", "exp"),
            P("ctx", "exp"),
            P("ctx", "exp"),
            P("ctx", "exp"),
            P("exp"),
            P("exp"),
            P("exp", "ctx"),
            P(),
            P("ctx", None),
            P("ctx", None),
            P("exp", None, "ctx"),
            P("exp", None, "ctx"),
            P("exp", "ctx", None),
        ),
        out_specs=(P(("ctx", "exp"), None), P("ctx", "exp", None, None)),
        check_vma=False,
    )
```

```python
import functools

import jax
import jax.numpy as jnp
from jax import lax
from jax.experimental import pallas as pl
from jax.experimental.pallas import tpu as pltpu
from jax.sharding import PartitionSpec as P

CHUNKS = 2
F32 = jnp.float32
BF16 = jnp.bfloat16
VMEM = pl.BlockSpec(memory_space=pltpu.VMEM)
SMEM = pl.BlockSpec(memory_space=pltpu.SMEM)
HBM = pl.BlockSpec(memory_space=pltpu.HBM)


def limit(mib):
    return pltpu.CompilerParams(vmem_limit_bytes=mib * 2**20)


def takes(us):
    return pl.CostEstimate(flops=int(us * 1e9), bytes_accessed=int(1e6), transcendentals=0)


def rows_iota(shape):
    return lax.broadcasted_iota(jnp.int32, shape, 0).astype(F32)


def cols_iota(shape):
    return lax.broadcasted_iota(jnp.int32, shape, 1).astype(F32)


def lanes(head, size):
    return pl.ds(pl.multiple_of(head * size, size), size)


def after(value, *others):
    return lax.optimization_barrier((value, *others))[0]


def state_kernel(per_half, place_ref, decay_ref, k_hbm, v_hbm, *refs):
    outs, (k_ref, v_ref, sems) = refs[: 2 * CHUNKS], refs[2 * CHUNKS :]
    pair = place_ref[0]
    tok, size = k_ref.shape[0], outs[0].shape[2]
    wide = k_ref.shape[1] // CHUNKS
    copies = []
    for chunk in range(CHUNKS):
        at = pl.ds(chunk * wide, wide)
        copies.append(
            [
                pltpu.make_async_copy(hbm.at[:, at], ref.at[:, at], sems.at[i, chunk])
                for i, (hbm, ref) in enumerate(((k_hbm, k_ref), (v_hbm, v_ref)))
            ]
        )
        for copy in copies[-1]:
            copy.start()
    back = (tok - 1.0) - rows_iota((tok, size))
    for chunk in range(CHUNKS):
        for copy in copies[chunk]:
            copy.wait()
        for which in (1, 0):
            half = pair if which == 0 else 1 - pair
            heads = [chunk * 2 * per_half + half * per_half + l for l in range(per_half)]
            keys = [
                (k_ref[:, lanes(h, size)].astype(F32) * jnp.exp(-decay_ref[h] * back)).astype(BF16)
                for h in heads
            ]
            states = [
                lax.dot_general(
                    k,
                    v_ref[:, lanes(h, size)],
                    (((0,), (0,)), ((), ())),
                    preferred_element_type=F32,
                )
                for k, h in zip(keys, heads)
            ]
            for l, state in enumerate(states):
                outs[chunk * 2 + which][l] = state.astype(BF16)


def near_kernel(chunk, heads, decay_ref, q_ref, k_ref, v_ref, gate_ref, gain_ref, near_ref, scale_ref, query_ref):
    tok = q_ref.shape[0]
    size = near_ref.shape[1] // heads
    gap = rows_iota((tok, tok)) - cols_iota((tok, tok))
    ahead = jnp.maximum(gap, 0.0)
    for first in range(0, heads, 4):
        local = range(first, min(first + 4, heads))
        at = [slice((chunk * heads + l) * size, (chunk * heads + l + 1) * size) for l in local]
        scores = [
            lax.dot_general(
                q_ref[:, s], k_ref[:, s], (((1,), (1,)), ((), ())), preferred_element_type=F32
            )
            for s in at
        ]
        weights = []
        for l, score in zip(local, scores):
            mask = jnp.where(gap >= 0.0, jnp.exp(-decay_ref[chunk * heads + l] * ahead), 0.0)
            weights.append((score * mask).astype(BF16))
        for l, s, w in zip(local, at, weights):
            near_ref[:, l * size : (l + 1) * size] = jnp.dot(
                w, v_ref[:, s], preferred_element_type=F32
            )
    own = slice(chunk * heads * size, (chunk + 1) * heads * size)
    gate = gate_ref[:, own].astype(F32)
    scale_ref[...] = gain_ref[:, own] / (1.0 + jnp.exp(-gate))
    query_ref[...] = q_ref[:, own]


def mix_kernel(
    chunk, per_half, own_rows, place_ref, decay_ref, q_ref, near_ref, scale_ref, mine_ref, other_ref, out_ref
):
    pair, own = place_ref[0], place_ref[1]
    size = mine_ref.shape[2]
    tok = q_ref.shape[0]
    ahead = rows_iota((tok, size)) + 1.0
    for which in range(2):
        prior = mine_ref if which == 0 else other_ref
        half = pair if which == 0 else 1 - pair
        local = [half * per_half + l for l in range(per_half)]
        far = [
            jnp.dot(q_ref[:, lanes(h, size)], prior[l], preferred_element_type=F32)
            for l, h in enumerate(local)
        ]
        mixed = []
        for h, part in zip(local, far):
            decay = decay_ref[chunk * 2 * per_half + h]
            attended = near_ref[:, lanes(h, size)] + part * jnp.exp(-decay * ahead)
            inverse = lax.rsqrt(jnp.mean(attended * attended, axis=1, keepdims=True) + 1e-06)
            mixed.append((attended * inverse * scale_ref[:, lanes(h, size)]).astype(BF16))
        for h, rows in zip(local, mixed):
            for block in range(tok // own_rows):
                to = pl.multiple_of((block ^ own) * own_rows, own_rows)
                out_ref[pl.ds(to, own_rows), lanes(h, size)] = rows[
                    block * own_rows : (block + 1) * own_rows
                ]


def project_kernel(n_exp, cap, token_ref, *refs):
    weight_ref, keep_ref, send_ref = refs[-3:]
    pairs = refs[:-3]
    chunks = len(pairs) // 2
    wide = pairs[0].shape[1]
    tok = pairs[0].shape[0]
    own_rows = tok // n_exp
    slots_of = []
    for y in range(2):
        total = None
        for chunk in range(chunks):
            part = jnp.dot(
                pairs[chunk * 2 + y][...],
                weight_ref[chunk * wide : (chunk + 1) * wide, :],
                preferred_element_type=F32,
            )
            total = part if total is None else total + part
        rows = total.astype(BF16)
        pick = token_ref[y] == lax.broadcasted_iota(jnp.int32, (n_exp * cap, tok), 1)
        slots = jnp.dot(pick.astype(F32).astype(BF16), rows, preferred_element_type=F32)
        for j in range(n_exp):
            out = send_ref if j % 2 else keep_ref
            out[j // 2, y * own_rows : (y + 1) * own_rows, :] = rows[j * own_rows : (j + 1) * own_rows]
        slots_of.append(slots)
    for j in range(n_exp):
        out = send_ref if j % 2 else keep_ref
        both = [s[j * cap : (j + 1) * cap] for s in slots_of]
        out[j // 2, 2 * own_rows :, :] = jnp.concatenate(both, axis=0).astype(BF16)


def hidden_kernel(cap, order_ref, stream_ref, *refs):
    out_ref, total_ref = refs[-2:]
    steps = (len(refs) - 2) // 2
    first = refs[0].shape[0] - 2 * cap
    for step in range(steps):
        rows = refs[2 * step][first:, :].astype(F32) + refs[2 * step + 1][first:, :].astype(F32)
        for y in range(2):
            to = pl.multiple_of(order_ref[2 * step + y] * cap, cap)
            total_ref[pl.ds(to, cap), :] = rows[y * cap : (y + 1) * cap]
    out_ref[...] = (total_ref[...] + stream_ref[...].astype(F32)).astype(BF16)


def ffn_kernel(n, blocks, order_ref, *refs):
    pieces, refs = refs[:n], refs[n:]
    gain_ref, refs = refs[0], refs[1:]
    gate_ref, up_ref, down_ref, out_ref, rows_ref, down_buf, sems = refs
    step = out_ref.shape[1] // blocks
    copies = [
        pltpu.make_async_copy(
            down_ref.at[0, :, pl.ds(i * step, step)], down_buf.at[i], sems.at[i]
        )
        for i in range(blocks)
    ]
    for copy in copies:
        copy.start()
    cols = pieces[0].shape[1]
    total = 0.0
    for piece in pieces:
        wide = piece[...].astype(F32)
        total = total + jnp.sum(wide * wide, axis=1, keepdims=True)
    inverse = lax.rsqrt(total * (1.0 / (n * cols)) + 1e-06)
    for i, piece in enumerate(pieces):
        at = lanes(order_ref[i], cols) if n > 1 else slice(None)
        rows_ref[:, at] = (piece[...].astype(F32) * inverse * gain_ref[:, at]).astype(BF16)
    gate = up = None
    span = rows_ref.shape[1] // blocks
    for i in range(blocks):
        rows = rows_ref[:, i * span : (i + 1) * span]
        g = jnp.dot(rows, gate_ref[0, i * span : (i + 1) * span, :], preferred_element_type=F32)
        u = jnp.dot(rows, up_ref[0, i * span : (i + 1) * span, :], preferred_element_type=F32)
        gate = g if gate is None else gate + g
        up = u if up is None else up + u
    activated = (gate / (1.0 + jnp.exp(-gate)) * up).astype(BF16)
    for i, copy in enumerate(copies):
        copy.wait()
        out_ref[:, i * step : (i + 1) * step] = jnp.dot(
            activated, down_buf[i], preferred_element_type=F32
        ).astype(BF16)


def per_device(
    stream_in,
    queries,
    key_proj,
    values,
    attn_gate,
    decay_rates,
    attn_gain,
    out_weight,
    ffn_gain,
    routing,
    route_weights,
    w_gate,
    w_up,
    w_down,
):
    tok, width = stream_in.shape
    heads = decay_rates.shape[0]
    size = queries.shape[1] // heads
    n_exp, n_ctx = lax.axis_size("exp"), lax.axis_size("ctx")
    own, place = lax.axis_index("exp"), lax.axis_index("ctx")
    groups = n_ctx // 2
    group, pair = place // 2, place % 2
    cap = tok // 16
    own_rows = tok // n_exp
    cols = out_weight.shape[1]
    hidden_units = w_gate.shape[2]
    per_half = heads // (2 * CHUNKS)
    per_chunk = heads // CHUNKS
    wide = per_chunk * size
    swap = [(i, i ^ 1) for i in range(n_ctx)]
    here = jnp.stack([pair, own]).astype(jnp.int32)

    def swapped(value):
        return lax.ppermute(value, "ctx", swap)

    def shifted(value, by):
        to = [(i, (i + 2 * by) % n_ctx) for i in range(n_ctx)]
        return lax.ppermute(value, "ctx", to)

    def in_hbm(value):
        return pltpu.with_memory_space_constraint(value, pltpu.HBM)

    states = pl.pallas_call(
        functools.partial(state_kernel, per_half),
        out_shape=[jax.ShapeDtypeStruct((per_half, size, size), BF16)] * (2 * CHUNKS),
        in_specs=[SMEM, SMEM, HBM, HBM],
        out_specs=[VMEM] * (2 * CHUNKS),
        scratch_shapes=[
            pltpu.VMEM((tok, heads * size), BF16),
            pltpu.VMEM((tok, heads * size), BF16),
            pltpu.SemaphoreType.DMA((2, CHUNKS)),
        ],
        compiler_params=limit(8),
        cost_estimate=takes(2),
        name="shard_state",
    )(here, decay_rates, in_hbm(key_proj), in_hbm(values))

    def near_part(chunk, start):
        return pl.pallas_call(
            functools.partial(near_kernel, chunk, per_chunk),
            out_shape=[
                jax.ShapeDtypeStruct((tok, wide), F32),
                jax.ShapeDtypeStruct((tok, wide), F32),
                jax.ShapeDtypeStruct((tok, wide), BF16),
            ],
            in_specs=[SMEM] + [VMEM] * 5,
            out_specs=[VMEM] * 3,
            compiler_params=limit(8),
            cost_estimate=takes(2),
            name="near_part",
        )(after(decay_rates, start), queries, key_proj, values, attn_gate, attn_gain[None, :])

    mixed, held = [], None
    for chunk in range(CHUNKS):
        keep, send = states[2 * chunk], states[2 * chunk + 1]
        got = swapped(send if held is None else after(send, held))
        near, scale, query = near_part(chunk, states[0] if held is None else held)
        first = chunk * per_chunk + pair * per_half
        rate = lax.dynamic_slice_in_dim(decay_rates, first, per_half, 0)[:, None, None]
        span = jnp.exp(-rate * tok)
        lower = jnp.where(pair == 0, keep, got).astype(F32)
        upper = jnp.where(pair == 0, got, keep).astype(F32)
        window = held = (span * lower + upper).astype(BF16)
        prior = jnp.zeros(lower.shape, F32)
        reach = 1
        while reach < groups:
            line = [(i, i + 2 * reach) for i in range(n_ctx - 2 * reach)]
            far = lax.ppermute(window, "ctx", line).astype(F32)
            prior = prior + jnp.exp(-rate * (2 * tok * (reach - 1))) * far
            window = (window.astype(F32) + jnp.exp(-rate * (2 * tok * reach)) * far).astype(BF16)
            reach *= 2
        second = span * prior + lower
        mine = jnp.where(pair == 0, prior, second).astype(BF16)
        other = swapped(jnp.where(pair == 0, second, prior).astype(BF16))
        mixed.append(
            pl.pallas_call(
                functools.partial(mix_kernel, chunk, per_half, own_rows),
                out_shape=jax.ShapeDtypeStruct((tok, wide), BF16),
                in_specs=[SMEM, SMEM] + [VMEM] * 5,
                out_specs=VMEM,
                compiler_params=limit(8),
                cost_estimate=takes(2),
                name="mix_heads",
            )(here, decay_rates, query, near, scale, mine, other)
        )

    routing = after(routing, mixed[0])
    hit = routing[:, :, None] == jnp.arange(n_exp, dtype=jnp.int32)
    member = jnp.any(hit, axis=1)
    gate_of = jnp.sum(jnp.where(hit, route_weights[:, :, None], 0.0), axis=1)
    position = jnp.arange(tok, dtype=jnp.int32)
    before = (position[:, None] > position[None, :]).astype(BF16)
    rank = jnp.dot(before, member.astype(BF16), preferred_element_type=F32)
    pick = member[:, :, None] & (rank[:, :, None] == jnp.arange(cap, dtype=F32))
    number = jnp.sum(jnp.where(pick, (position + 1).astype(F32)[:, None, None], 0.0), axis=0)
    own_pick = lax.dynamic_index_in_dim(pick, own, 1, keepdims=False)
    own_weight = jnp.sum(
        jnp.where(own_pick, lax.dynamic_index_in_dim(gate_of, own, 1), 0.0), axis=0
    )
    stream_slots = lax.dot_general(
        own_pick.astype(BF16), stream_in, (((0,), (0,)), ((), ())), preferred_element_type=F32
    ).astype(BF16)
    parcel = stream_slots.reshape(cap, n_ctx, cols).transpose(1, 0, 2)
    label = jnp.pad(number.reshape(1, n_exp * cap), ((0, cap - 1), (0, cols - n_exp * cap)))
    label = jnp.broadcast_to(label.astype(BF16)[None], (n_ctx, cap, cols))
    parcel = jnp.concatenate([parcel, label], axis=1)

    arrived = lax.all_to_all(parcel, "ctx", split_axis=0, concat_axis=0, tiled=True)
    stream_rows = arrived[:, :cap].reshape(n_ctx * cap, cols)
    token = arrived[:, cap, : n_exp * cap].astype(jnp.int32).reshape(n_ctx, n_exp, cap) - 1
    token = jnp.where(token >= 0, ((token // own_rows) ^ own) * own_rows + token % own_rows, -1)
    token = jnp.stack(
        [lax.dynamic_index_in_dim(token, own ^ j, 1, keepdims=False) for j in range(n_exp)], axis=1
    )
    index = jnp.arange(n_ctx, dtype=jnp.int32)
    order = ((group - index // 2) % groups) * 2 + (pair ^ (index % 2))
    token = jnp.take(token, order, axis=0).reshape(n_ctx, n_exp * cap, 1)

    rows_of = [[[], []] for _ in range(groups)]
    for chunk in range(CHUNKS):
        current, crossed = mixed[chunk], None
        for step in range(groups):
            crossed = shifted(crossed, 1) if chunk % 2 and step == 1 else swapped(current)
            rows_of[step][0].append(current)
            rows_of[step][1].append(crossed)
            if step + 1 < groups:
                current = shifted(current, 1)
    kept, got = [], []
    for step in range(groups):
        out = jax.ShapeDtypeStruct((n_exp // 2, 2 * (own_rows + cap), cols), BF16)
        keep, send = pl.pallas_call(
            functools.partial(project_kernel, n_exp, cap),
            out_shape=[out, out],
            in_specs=[VMEM] * (2 + 2 * CHUNKS),
            out_specs=[VMEM] * 2,
            compiler_params=limit(8),
            cost_estimate=takes(8),
            name="project",
        )(
            token[2 * step : 2 * step + 2],
            *[rows_of[step][y][chunk] for chunk in range(CHUNKS) for y in range(2)],
            out_weight,
        )
        came = lax.ppermute(send, "exp", [(i, i ^ 1) for i in range(n_exp)])
        bit = 2
        while bit < n_exp:
            total = (keep.astype(F32) + came.astype(F32)).astype(BF16)
            total = total.reshape(n_exp // (2 * bit), 2, *total.shape[1:])
            keep = total[:, 0]
            came = lax.ppermute(total[:, 1], "exp", [(i, i ^ bit) for i in range(n_exp)])
            bit *= 2
        kept.append(keep[0])
        got.append(came[0])
    hidden = pl.pallas_call(
        functools.partial(hidden_kernel, cap),
        out_shape=jax.ShapeDtypeStruct((n_ctx * cap, cols), BF16),
        in_specs=[SMEM] + [VMEM] * (1 + 2 * groups),
        out_specs=VMEM,
        scratch_shapes=[pltpu.VMEM((n_ctx * cap, cols), F32)],
        compiler_params=limit(8),
        cost_estimate=takes(1),
        name="slot_hidden",
    )(order, stream_rows, *[part for pair_of in zip(kept, got) for part in pair_of])

    pieces = {0: hidden}
    bit = 1
    while bit < groups:
        for r in range(bit):
            pieces[r | bit] = lax.ppermute(
                pieces[r], "ctx", [(i, i ^ (2 * bit)) for i in range(n_ctx)]
            )
        bit *= 2
    pieces = [p for r in range(groups) for p in (pieces[r], swapped(pieces[r]))]
    source = (place ^ index).astype(jnp.int32)
    if cols % 128:
        pieces = [jnp.take(jnp.stack(pieces), source, axis=0).transpose(1, 0, 2).reshape(-1, width)]

    bulk = [
        (k.astype(F32) + g.astype(F32))[: 2 * own_rows].astype(BF16).reshape(2, own_rows, cols)
        for k, g in zip(kept, got)
    ]
    back = []
    for step in range(groups):
        rows = jnp.stack([bulk[step][0], swapped(after(bulk[step][1], hidden))])
        back.append(shifted(rows, -step) if step else rows)

    blocks = 8
    down = pl.pallas_call(
        functools.partial(ffn_kernel, len(pieces), blocks),
        out_shape=jax.ShapeDtypeStruct((n_ctx * cap, width), BF16),
        in_specs=[SMEM] + [VMEM] * (len(pieces) + 3) + [HBM],
        out_specs=VMEM,
        scratch_shapes=[
            pltpu.VMEM((n_ctx * cap, width), BF16),
            pltpu.VMEM((blocks, hidden_units, width // blocks), BF16),
            pltpu.SemaphoreType.DMA((blocks,)),
        ],
        compiler_params=limit(24),
        cost_estimate=takes(10),
        name="expert",
    )(source, *pieces, ffn_gain[None, :], w_gate, w_up, in_hbm(w_down))
    down = after(down, *back)
    received = lax.all_to_all(
        down.reshape(n_ctx, cap, width), "ctx", split_axis=0, concat_axis=0, tiled=True
    )
    summed = jnp.sum(received.astype(F32), axis=0)
    expert_out = (summed * own_weight[:, None]).astype(BF16).reshape(1, 1, cap, width)

    order = ((index // 2 - group) % groups) * 2 + (pair ^ (index % 2))
    projected = jnp.take(jnp.concatenate(back), order, axis=0).transpose(1, 0, 2)
    projected = projected.reshape(own_rows, width)
    stream_own = lax.dynamic_slice_in_dim(stream_in, own * own_rows, own_rows, 0)
    residual_out = (stream_own.astype(F32) + projected.astype(F32)).astype(BF16)
    return (residual_out, expert_out)


def solution(mesh):
    return jax.shard_map(
        per_device,
        mesh=mesh,
        in_specs=(
            P("ctx", None),
            P("ctx", "exp"),
            P("ctx", "exp"),
            P("ctx", "exp"),
            P("ctx", "exp"),
            P("exp"),
            P("exp"),
            P("exp", "ctx"),
            P(),
            P("ctx", None),
            P("ctx", None),
            P("exp", None, "ctx"),
            P("exp", None, "ctx"),
            P("exp", "ctx", None),
        ),
        out_specs=(P(("ctx", "exp"), None), P("ctx", "exp", None, None)),
        check_vma=False,
    )
```

```python
import functools

import jax
import jax.numpy as jnp
from jax import lax
from jax.experimental import pallas as pl
from jax.experimental.pallas import tpu as pltpu
from jax.sharding import PartitionSpec as P

CHUNKS = 2
F32 = jnp.float32
BF16 = jnp.bfloat16
VMEM = pl.BlockSpec(memory_space=pltpu.VMEM)
SMEM = pl.BlockSpec(memory_space=pltpu.SMEM)
HBM = pl.BlockSpec(memory_space=pltpu.HBM)


def limit(mib):
    return pltpu.CompilerParams(vmem_limit_bytes=mib * 2**20)


def takes(us):
    return pl.CostEstimate(flops=int(us * 1e9), bytes_accessed=int(1e6), transcendentals=0)


def rows_iota(shape):
    return lax.broadcasted_iota(jnp.int32, shape, 0).astype(F32)


def cols_iota(shape):
    return lax.broadcasted_iota(jnp.int32, shape, 1).astype(F32)


def lanes(head, size):
    return pl.ds(pl.multiple_of(head * size, size), size)


def after(value, *others):
    return lax.optimization_barrier((value, *others))[0]


def state_kernel(per_half, place_ref, decay_ref, k_hbm, v_hbm, *refs):
    outs, (k_ref, v_ref, sems) = refs[: 2 * CHUNKS], refs[2 * CHUNKS :]
    pair = place_ref[0]
    tok, size = k_ref.shape[0], outs[0].shape[2]
    wide = k_ref.shape[1] // CHUNKS
    copies = []
    for chunk in range(CHUNKS):
        at = pl.ds(chunk * wide, wide)
        copies.append(
            [
                pltpu.make_async_copy(hbm.at[:, at], ref.at[:, at], sems.at[i, chunk])
                for i, (hbm, ref) in enumerate(((k_hbm, k_ref), (v_hbm, v_ref)))
            ]
        )
        for copy in copies[-1]:
            copy.start()
    back = (tok - 1.0) - rows_iota((tok, size))
    for chunk in range(CHUNKS):
        for copy in copies[chunk]:
            copy.wait()
        for which in (1, 0):
            half = pair if which == 0 else 1 - pair
            heads = [chunk * 2 * per_half + half * per_half + l for l in range(per_half)]
            keys = [
                (k_ref[:, lanes(h, size)].astype(F32) * jnp.exp(-decay_ref[h] * back)).astype(BF16)
                for h in heads
            ]
            states = [
                lax.dot_general(
                    k,
                    v_ref[:, lanes(h, size)],
                    (((0,), (0,)), ((), ())),
                    preferred_element_type=F32,
                )
                for k, h in zip(keys, heads)
            ]
            for l, state in enumerate(states):
                outs[chunk * 2 + which][l] = state.astype(BF16)


def near_kernel(chunk, heads, decay_ref, q_ref, k_ref, v_ref, gate_ref, gain_ref, near_ref, scale_ref, query_ref):
    tok = q_ref.shape[0]
    size = near_ref.shape[1] // heads
    gap = rows_iota((tok, tok)) - cols_iota((tok, tok))
    ahead = jnp.maximum(gap, 0.0)
    for first in range(0, heads, 4):
        local = range(first, min(first + 4, heads))
        at = [slice((chunk * heads + l) * size, (chunk * heads + l + 1) * size) for l in local]
        scores = [
            lax.dot_general(
                q_ref[:, s], k_ref[:, s], (((1,), (1,)), ((), ())), preferred_element_type=F32
            )
            for s in at
        ]
        weights = []
        for l, score in zip(local, scores):
            mask = jnp.where(gap >= 0.0, jnp.exp(-decay_ref[chunk * heads + l] * ahead), 0.0)
            weights.append((score * mask).astype(BF16))
        for l, s, w in zip(local, at, weights):
            near_ref[:, l * size : (l + 1) * size] = jnp.dot(
                w, v_ref[:, s], preferred_element_type=F32
            )
    own = slice(chunk * heads * size, (chunk + 1) * heads * size)
    gate = gate_ref[:, own].astype(F32)
    scale_ref[...] = gain_ref[:, own] / (1.0 + jnp.exp(-gate))
    query_ref[...] = q_ref[:, own]


def mix_kernel(
    chunk, per_half, own_rows, place_ref, decay_ref, q_ref, near_ref, scale_ref, mine_ref, other_ref, out_ref
):
    pair, own = place_ref[0], place_ref[1]
    size = mine_ref.shape[2]
    tok = q_ref.shape[0]
    ahead = rows_iota((tok, size)) + 1.0
    for which in range(2):
        prior = mine_ref if which == 0 else other_ref
        half = pair if which == 0 else 1 - pair
        local = [half * per_half + l for l in range(per_half)]
        far = [
            jnp.dot(q_ref[:, lanes(h, size)], prior[l], preferred_element_type=F32)
            for l, h in enumerate(local)
        ]
        mixed = []
        for h, part in zip(local, far):
            decay = decay_ref[chunk * 2 * per_half + h]
            attended = near_ref[:, lanes(h, size)] + part * jnp.exp(-decay * ahead)
            inverse = lax.rsqrt(jnp.mean(attended * attended, axis=1, keepdims=True) + 1e-06)
            mixed.append((attended * inverse * scale_ref[:, lanes(h, size)]).astype(BF16))
        for h, rows in zip(local, mixed):
            for block in range(tok // own_rows):
                to = pl.multiple_of((block ^ own) * own_rows, own_rows)
                out_ref[pl.ds(to, own_rows), lanes(h, size)] = rows[
                    block * own_rows : (block + 1) * own_rows
                ]


def project_kernel(n_exp, *refs):
    weight_ref, outs = refs[-3], refs[-2:]
    pairs = refs[:-3]
    chunks = len(pairs) // 2
    wide = pairs[0].shape[1]
    own_rows = pairs[0].shape[0] // n_exp
    for y in range(2):
        total = None
        for chunk in range(chunks):
            part = jnp.dot(
                pairs[chunk * 2 + y][...],
                weight_ref[chunk * wide : (chunk + 1) * wide, :],
                preferred_element_type=F32,
            )
            total = part if total is None else total + part
        rows = total.astype(BF16)
        for j in range(n_exp):
            outs[j % 2][j // 2, y * own_rows : (y + 1) * own_rows, :] = rows[
                j * own_rows : (j + 1) * own_rows
            ]


def select_kernel(n_exp, cap, row_ref, *refs):
    parts, outs = refs[:-2], refs[-2:]
    for step in range(len(parts) // 2):
        both = parts[2 * step : 2 * step + 2]
        rows = jnp.concatenate([p[i] for p in both for i in range(n_exp // 2)], axis=0)
        slots = n_exp * 2 * cap
        pick = row_ref[step] == lax.broadcasted_iota(jnp.int32, (slots, rows.shape[0]), 1)
        found = jnp.dot(pick.astype(F32).astype(BF16), rows, preferred_element_type=F32)
        found = found.astype(BF16)
        for j in range(n_exp):
            outs[j % 2][j // 2, 2 * cap * step : 2 * cap * (step + 1), :] = found[
                2 * cap * j : 2 * cap * (j + 1)
            ]


def hidden_kernel(cap, order_ref, stream_ref, mine_ref, came_ref, out_ref, total_ref):
    rows = mine_ref[...].astype(F32) + came_ref[...].astype(F32)
    for i in range(rows.shape[0] // cap):
        to = pl.multiple_of(order_ref[i] * cap, cap)
        total_ref[pl.ds(to, cap), :] = rows[i * cap : (i + 1) * cap]
    out_ref[...] = (total_ref[...] + stream_ref[...].astype(F32)).astype(BF16)


def ffn_kernel(n, blocks, order_ref, *refs):
    pieces, refs = refs[:n], refs[n:]
    gain_ref, gate_ref, up_ref, down_ref, out_ref, rows_ref, up_buf, down_buf, sems = refs
    rows_step = up_buf.shape[1]
    step = out_ref.shape[1] // blocks
    ups = [
        pltpu.make_async_copy(
            up_ref.at[0, pl.ds(i * rows_step, rows_step), :], up_buf.at[i], sems.at[0, i]
        )
        for i in range(blocks)
    ]
    downs = [
        pltpu.make_async_copy(
            down_ref.at[0, :, pl.ds(i * step, step)], down_buf.at[i], sems.at[1, i]
        )
        for i in range(blocks)
    ]
    for copy in ups + downs:
        copy.start()
    cols = pieces[0].shape[1]
    total = 0.0
    for piece in pieces:
        wide = piece[...].astype(F32)
        total = total + jnp.sum(wide * wide, axis=1, keepdims=True)
    inverse = lax.rsqrt(total * (1.0 / (n * cols)) + 1e-06)
    for i, piece in enumerate(pieces):
        at = lanes(order_ref[i], cols) if n > 1 else slice(None)
        rows_ref[:, at] = (piece[...].astype(F32) * inverse * gain_ref[:, at]).astype(BF16)
    spans = [slice(i * rows_step, (i + 1) * rows_step) for i in range(blocks)]
    gate = up = None
    for at in spans:
        g = jnp.dot(rows_ref[:, at], gate_ref[0, at, :], preferred_element_type=F32)
        gate = g if gate is None else gate + g
    gate = gate / (1.0 + jnp.exp(-gate))
    for i, at in enumerate(spans):
        ups[i].wait()
        u = jnp.dot(rows_ref[:, at], up_buf[i], preferred_element_type=F32)
        up = u if up is None else up + u
    activated = (gate * up).astype(BF16)
    for i, copy in enumerate(downs):
        copy.wait()
        out_ref[:, i * step : (i + 1) * step] = jnp.dot(
            activated, down_buf[i], preferred_element_type=F32
        ).astype(BF16)


def per_device(
    stream_in,
    queries,
    key_proj,
    values,
    attn_gate,
    decay_rates,
    attn_gain,
    out_weight,
    ffn_gain,
    routing,
    route_weights,
    w_gate,
    w_up,
    w_down,
):
    tok, width = stream_in.shape
    heads = decay_rates.shape[0]
    size = queries.shape[1] // heads
    n_exp, n_ctx = lax.axis_size("exp"), lax.axis_size("ctx")
    own, place = lax.axis_index("exp"), lax.axis_index("ctx")
    groups = n_ctx // 2
    group, pair = place // 2, place % 2
    cap = tok // 16
    own_rows = tok // n_exp
    cols = out_weight.shape[1]
    hidden_units = w_gate.shape[2]
    per_half = heads // (2 * CHUNKS)
    per_chunk = heads // CHUNKS
    wide = per_chunk * size
    swap = [(i, i ^ 1) for i in range(n_ctx)]
    here = jnp.stack([pair, own]).astype(jnp.int32)

    def swapped(value):
        return lax.ppermute(value, "ctx", swap)

    def shifted(value, by):
        to = [(i, (i + 2 * by) % n_ctx) for i in range(n_ctx)]
        return lax.ppermute(value, "ctx", to)

    def in_hbm(value):
        return pltpu.with_memory_space_constraint(value, pltpu.HBM)

    states = pl.pallas_call(
        functools.partial(state_kernel, per_half),
        out_shape=[jax.ShapeDtypeStruct((per_half, size, size), BF16)] * (2 * CHUNKS),
        in_specs=[SMEM, SMEM, HBM, HBM],
        out_specs=[VMEM] * (2 * CHUNKS),
        scratch_shapes=[
            pltpu.VMEM((tok, heads * size), BF16),
            pltpu.VMEM((tok, heads * size), BF16),
            pltpu.SemaphoreType.DMA((2, CHUNKS)),
        ],
        compiler_params=limit(8),
        cost_estimate=takes(1),
        name="shard_state",
    )(here, decay_rates, in_hbm(key_proj), in_hbm(values))

    def near_part(chunk, start):
        return pl.pallas_call(
            functools.partial(near_kernel, chunk, per_chunk),
            out_shape=[
                jax.ShapeDtypeStruct((tok, wide), F32),
                jax.ShapeDtypeStruct((tok, wide), F32),
                jax.ShapeDtypeStruct((tok, wide), BF16),
            ],
            in_specs=[SMEM] + [VMEM] * 5,
            out_specs=[VMEM] * 3,
            compiler_params=limit(8),
            cost_estimate=takes(1),
            name="near_part",
        )(after(decay_rates, start), queries, key_proj, values, attn_gate, attn_gain[None, :])

    routing = after(routing, states[0])
    hit = routing[:, :, None] == jnp.arange(n_exp, dtype=jnp.int32)
    member = jnp.any(hit, axis=1)
    gate_of = jnp.sum(jnp.where(hit, route_weights[:, :, None], 0.0), axis=1)
    position = jnp.arange(tok, dtype=jnp.int32)
    before = (position[:, None] > position[None, :]).astype(BF16)
    rank = jnp.dot(before, member.astype(BF16), preferred_element_type=F32)
    pick = member[:, :, None] & (rank[:, :, None] == jnp.arange(cap, dtype=F32))
    number = jnp.sum(jnp.where(pick, (position + 1).astype(F32)[:, None, None], 0.0), axis=0)
    own_pick = lax.dynamic_index_in_dim(pick, own, 1, keepdims=False)
    own_weight = jnp.sum(
        jnp.where(own_pick, lax.dynamic_index_in_dim(gate_of, own, 1), 0.0), axis=0
    )
    stream_slots = lax.dot_general(
        own_pick.astype(BF16), stream_in, (((0,), (0,)), ((), ())), preferred_element_type=F32
    ).astype(BF16)
    parcel = stream_slots.reshape(cap, n_ctx, cols).transpose(1, 0, 2)
    label = jnp.pad(number.reshape(1, n_exp * cap), ((0, cap - 1), (0, cols - n_exp * cap)))
    label = jnp.broadcast_to(label.astype(BF16)[None], (n_ctx, cap, cols))
    parcel = jnp.concatenate([parcel, label], axis=1)


    mixed, held = [], None
    for chunk in range(CHUNKS):
        keep, send = states[2 * chunk], states[2 * chunk + 1]
        got = swapped(send if held is None else after(send, held))
        first = chunk * per_chunk + pair * per_half
        rate = lax.dynamic_slice_in_dim(decay_rates, first, per_half, 0)[:, None, None]
        span = jnp.exp(-rate * tok)
        lower = jnp.where(pair == 0, keep, got).astype(F32)
        upper = jnp.where(pair == 0, got, keep).astype(F32)
        window = held = (span * lower + upper).astype(BF16)
        prior = jnp.zeros(lower.shape, F32)
        reach = 1
        while reach < groups:
            line = [(i, i + 2 * reach) for i in range(n_ctx - 2 * reach)]
            far = lax.ppermute(window, "ctx", line).astype(F32)
            prior = prior + jnp.exp(-rate * (2 * tok * (reach - 1))) * far
            window = (window.astype(F32) + jnp.exp(-rate * (2 * tok * reach)) * far).astype(BF16)
            reach *= 2
        near, scale, query = near_part(chunk, far)
        second = span * prior + lower
        mine = jnp.where(pair == 0, prior, second).astype(BF16)
        if chunk == 0:
            mine = after(mine, parcel)
        other = swapped(jnp.where(pair == 0, second, prior).astype(BF16))
        mixed.append(
            pl.pallas_call(
                functools.partial(mix_kernel, chunk, per_half, own_rows),
                out_shape=jax.ShapeDtypeStruct((tok, wide), BF16),
                in_specs=[SMEM, SMEM] + [VMEM] * 5,
                out_specs=VMEM,
                compiler_params=limit(8),
                cost_estimate=takes(1),
                name="mix_heads",
            )(here, decay_rates, query, near, scale, mine, other)
        )

    ring = [[m] for m in mixed]
    cross = [[None] * groups for _ in mixed]
    swaps = []
    for step in range(groups):
        for chunk in range(CHUNKS):
            if step + 1 < groups:
                ring[chunk].append(shifted(ring[chunk][step], 1))
        for chunk in range(CHUNKS):
            if chunk % 2 == 0 or step != 1:
                held = swaps[-2:-1] if len(swaps) > 1 else []
                cross[chunk][step] = swapped(after(ring[chunk][step], *held))
                swaps.append(cross[chunk][step])
    for chunk in range(1, CHUNKS, 2):
        cross[chunk][1] = shifted(after(cross[chunk][0], ring[chunk - 1][-1]), 1)
    rows_of = [
        [[r[step] for r in ring], [c[step] for c in cross]] for step in range(groups)
    ]

    arrived = lax.all_to_all(
        after(parcel, ring[0][-1]), "ctx", split_axis=0, concat_axis=0, tiled=True
    )
    stream_rows = arrived[:, :cap].reshape(n_ctx * cap, cols)
    token = arrived[:, cap, : n_exp * cap].astype(jnp.int32).reshape(n_ctx, n_exp, cap) - 1
    index = jnp.arange(n_ctx, dtype=jnp.int32)
    order = ((group - index // 2) % groups) * 2 + (pair ^ (index % 2))
    turned = (token // own_rows) ^ own
    row = (turned % 2 * (n_exp // 2) + turned // 2) * 2 + (index % 2 ^ pair)[:, None, None]
    row = jnp.where(token >= 0, row * own_rows + token % own_rows, -1)
    row = jnp.stack(
        [lax.dynamic_index_in_dim(row, own ^ j, 1, keepdims=False) for j in range(n_exp)], axis=1
    )
    row = jnp.take(row, order, axis=0).reshape(groups, 2, n_exp, cap)
    row = row.transpose(0, 2, 1, 3).reshape(groups, n_exp * 2 * cap, 1)

    parts = []
    for step in range(groups):
        weight = out_weight
        if step + 1 < groups:
            weight = after(weight, cross[0][-1])
        rows = jax.ShapeDtypeStruct((n_exp // 2, 2 * own_rows, cols), BF16)
        parts.append(
            pl.pallas_call(
                functools.partial(project_kernel, n_exp),
                out_shape=[rows, rows],
                in_specs=[VMEM] * (1 + 2 * CHUNKS),
                out_specs=[VMEM] * 2,
                compiler_params=limit(8),
                cost_estimate=takes(1.5),
                name="project",
            )(*[rows_of[step][y][chunk] for chunk in range(CHUNKS) for y in range(2)], weight)
        )
    slots = jax.ShapeDtypeStruct((n_exp // 2, n_ctx * cap, cols), BF16)
    slot_parts = pl.pallas_call(
        functools.partial(select_kernel, n_exp, cap),
        out_shape=[slots, slots],
        in_specs=[VMEM] * (1 + 2 * groups),
        out_specs=[VMEM] * 2,
        compiler_params=limit(8),
        cost_estimate=takes(1),
        name="slot_rows",
    )(row, *[p for both in parts for p in both])

    def add_groups(keep, send):
        came = lax.ppermute(send, "exp", [(i, i ^ 1) for i in range(n_exp)])
        bit = 2
        while bit < n_exp:
            total = (keep.astype(F32) + came.astype(F32)).astype(BF16)
            total = total.reshape(n_exp // (2 * bit), 2, *total.shape[1:])
            keep = total[:, 0]
            came = lax.ppermute(total[:, 1], "exp", [(i, i ^ bit) for i in range(n_exp)])
            bit *= 2
        return keep[0], came[0]

    hidden = pl.pallas_call(
        functools.partial(hidden_kernel, cap),
        out_shape=jax.ShapeDtypeStruct((n_ctx * cap, cols), BF16),
        in_specs=[SMEM] + [VMEM] * 3,
        out_specs=VMEM,
        scratch_shapes=[pltpu.VMEM((n_ctx * cap, cols), F32)],
        compiler_params=limit(8),
        cost_estimate=takes(15),
        name="slot_hidden",
    )(order, stream_rows, *add_groups(*slot_parts))

    pieces = {0: hidden}
    bit = 1
    while bit < groups:
        for r in range(bit):
            pieces[r | bit] = lax.ppermute(
                pieces[r], "ctx", [(i, i ^ (2 * bit)) for i in range(n_ctx)]
            )
        bit *= 2
    pieces = [p for r in range(groups) for p in (pieces[r], swapped(pieces[r]))]
    late = pieces[-3:-1]
    source = (place ^ index).astype(jnp.int32)
    if cols % 128:
        pieces = [jnp.take(jnp.stack(pieces), source, axis=0).transpose(1, 0, 2).reshape(-1, width)]

    bulk_parts = [jnp.concatenate([p[i] for p in parts], axis=1) for i in (0, 1)]
    mine, came = add_groups(bulk_parts[0], after(bulk_parts[1], *late))
    bulk = (mine.astype(F32) + came.astype(F32)).astype(BF16)
    bulk = bulk.reshape(groups, 2, own_rows, cols)

    blocks = 8
    down = pl.pallas_call(
        functools.partial(ffn_kernel, len(pieces), blocks),
        out_shape=jax.ShapeDtypeStruct((n_ctx * cap, width), BF16),
        in_specs=[SMEM] + [VMEM] * (len(pieces) + 2) + [HBM, HBM],
        out_specs=VMEM,
        scratch_shapes=[
            pltpu.VMEM((n_ctx * cap, width), BF16),
            pltpu.VMEM((blocks, width // blocks, hidden_units), BF16),
            pltpu.VMEM((blocks, hidden_units, width // blocks), BF16),
            pltpu.SemaphoreType.DMA((2, blocks)),
        ],
        compiler_params=limit(36),
        cost_estimate=takes(10),
        name="expert",
    )(source, *pieces, ffn_gain[None, :], w_gate, in_hbm(w_up), in_hbm(w_down))
    received = lax.all_to_all(
        down.reshape(n_ctx, cap, width), "ctx", split_axis=0, concat_axis=0, tiled=True
    )
    summed = jnp.sum(received.astype(F32), axis=0)
    expert_out = (summed * own_weight[:, None]).astype(BF16).reshape(1, 1, cap, width)

    turned = jnp.stack([bulk[:, 0], swapped(bulk[:, 1])], axis=1)
    back = [turned[0]] + [shifted(turned[k], -k) for k in range(1, groups)]
    order = ((index // 2 - group) % groups) * 2 + (pair ^ (index % 2))
    projected = jnp.take(jnp.concatenate(back), order, axis=0).transpose(1, 0, 2)
    projected = projected.reshape(own_rows, width)
    stream_own = lax.dynamic_slice_in_dim(stream_in, own * own_rows, own_rows, 0)
    residual_out = (stream_own.astype(F32) + projected.astype(F32)).astype(BF16)
    return (residual_out, expert_out)


def solution(mesh):
    return jax.shard_map(
        per_device,
        mesh=mesh,
        in_specs=(
            P("ctx", None),
            P("ctx", "exp"),
            P("ctx", "exp"),
            P("ctx", "exp"),
            P("ctx", "exp"),
            P("exp"),
            P("exp"),
            P("exp", "ctx"),
            P(),
            P("ctx", None),
            P("ctx", None),
            P("exp", None, "ctx"),
            P("exp", None, "ctx"),
            P("exp", "ctx", None),
        ),
        out_specs=(P(("ctx", "exp"), None), P("ctx", "exp", None, None)),
        check_vma=False,
    )
```

```python
import functools

import jax
import jax.numpy as jnp
from jax import lax
from jax.experimental import pallas as pl
from jax.experimental.pallas import tpu as pltpu
from jax.sharding import PartitionSpec as P

CHUNKS = 2
F32 = jnp.float32
BF16 = jnp.bfloat16
VMEM = pl.BlockSpec(memory_space=pltpu.VMEM)
SMEM = pl.BlockSpec(memory_space=pltpu.SMEM)
HBM = pl.BlockSpec(memory_space=pltpu.HBM)


def limit(mib):
    return pltpu.CompilerParams(vmem_limit_bytes=mib * 2**20)


def takes(us):
    return pl.CostEstimate(flops=int(us * 1e9), bytes_accessed=int(1e6), transcendentals=0)


def rows_iota(shape):
    return lax.broadcasted_iota(jnp.int32, shape, 0).astype(F32)


def cols_iota(shape):
    return lax.broadcasted_iota(jnp.int32, shape, 1).astype(F32)


def lanes(head, size):
    return pl.ds(pl.multiple_of(head * size, size), size)


def after(value, *others):
    return lax.optimization_barrier((value, *others))[0]


def state_kernel(per_half, place_ref, decay_ref, k_hbm, v_hbm, *refs):
    outs, (k_ref, v_ref, sems) = refs[: 2 * CHUNKS], refs[2 * CHUNKS :]
    pair = place_ref[0]
    tok, size = k_ref.shape[0], outs[0].shape[2]
    wide = k_ref.shape[1] // CHUNKS
    copies = []
    for chunk in range(CHUNKS):
        at = pl.ds(chunk * wide, wide)
        copies.append(
            [
                pltpu.make_async_copy(hbm.at[:, at], ref.at[:, at], sems.at[i, chunk])
                for i, (hbm, ref) in enumerate(((k_hbm, k_ref), (v_hbm, v_ref)))
            ]
        )
        for copy in copies[-1]:
            copy.start()
    back = (tok - 1.0) - rows_iota((tok, size))
    for chunk in range(CHUNKS):
        for copy in copies[chunk]:
            copy.wait()
        for which in (1, 0):
            half = pair if which == 0 else 1 - pair
            heads = [chunk * 2 * per_half + half * per_half + l for l in range(per_half)]
            keys = [
                (k_ref[:, lanes(h, size)].astype(F32) * jnp.exp(-decay_ref[h] * back)).astype(BF16)
                for h in heads
            ]
            states = [
                lax.dot_general(
                    k,
                    v_ref[:, lanes(h, size)],
                    (((0,), (0,)), ((), ())),
                    preferred_element_type=F32,
                )
                for k, h in zip(keys, heads)
            ]
            for l, state in enumerate(states):
                outs[chunk * 2 + which][l] = state.astype(BF16)


def near_kernel(chunk, heads, decay_ref, q_ref, k_ref, v_ref, gate_ref, gain_ref, near_ref, scale_ref, query_ref):
    tok = q_ref.shape[0]
    size = near_ref.shape[1] // heads
    gap = rows_iota((tok, tok)) - cols_iota((tok, tok))
    ahead = jnp.maximum(gap, 0.0)
    for first in range(0, heads, 4):
        local = range(first, min(first + 4, heads))
        at = [slice((chunk * heads + l) * size, (chunk * heads + l + 1) * size) for l in local]
        scores = [
            lax.dot_general(
                q_ref[:, s], k_ref[:, s], (((1,), (1,)), ((), ())), preferred_element_type=F32
            )
            for s in at
        ]
        weights = []
        for l, score in zip(local, scores):
            mask = jnp.where(gap >= 0.0, jnp.exp(-decay_ref[chunk * heads + l] * ahead), 0.0)
            weights.append((score * mask).astype(BF16))
        for l, s, w in zip(local, at, weights):
            near_ref[:, l * size : (l + 1) * size] = jnp.dot(
                w, v_ref[:, s], preferred_element_type=F32
            )
    own = slice(chunk * heads * size, (chunk + 1) * heads * size)
    gate = gate_ref[:, own].astype(F32)
    scale_ref[...] = gain_ref[:, own] / (1.0 + jnp.exp(-gate))
    query_ref[...] = q_ref[:, own]


def mix_kernel(
    chunk, per_half, own_rows, place_ref, decay_ref, q_ref, near_ref, scale_ref, mine_ref, other_ref, out_ref
):
    pair, own = place_ref[0], place_ref[1]
    size = mine_ref.shape[2]
    tok = q_ref.shape[0]
    ahead = rows_iota((tok, size)) + 1.0
    for which in range(2):
        prior = mine_ref if which == 0 else other_ref
        half = pair if which == 0 else 1 - pair
        local = [half * per_half + l for l in range(per_half)]
        far = [
            jnp.dot(q_ref[:, lanes(h, size)], prior[l], preferred_element_type=F32)
            for l, h in enumerate(local)
        ]
        mixed = []
        for h, part in zip(local, far):
            decay = decay_ref[chunk * 2 * per_half + h]
            attended = near_ref[:, lanes(h, size)] + part * jnp.exp(-decay * ahead)
            inverse = lax.rsqrt(jnp.mean(attended * attended, axis=1, keepdims=True) + 1e-06)
            mixed.append((attended * inverse * scale_ref[:, lanes(h, size)]).astype(BF16))
        for h, rows in zip(local, mixed):
            for block in range(tok // own_rows):
                to = pl.multiple_of((block ^ own) * own_rows, own_rows)
                out_ref[pl.ds(to, own_rows), lanes(h, size)] = rows[
                    block * own_rows : (block + 1) * own_rows
                ]


def project_kernel(n_exp, *refs):
    weight_ref, outs = refs[-3], refs[-2:]
    pairs = refs[:-3]
    chunks = len(pairs) // 2
    wide = pairs[0].shape[1]
    own_rows = pairs[0].shape[0] // n_exp
    for y in range(2):
        total = None
        for chunk in range(chunks):
            part = jnp.dot(
                pairs[chunk * 2 + y][...],
                weight_ref[chunk * wide : (chunk + 1) * wide, :],
                preferred_element_type=F32,
            )
            total = part if total is None else total + part
        rows = total.astype(BF16)
        for j in range(n_exp):
            outs[j % 2][j // 2, y * own_rows : (y + 1) * own_rows, :] = rows[
                j * own_rows : (j + 1) * own_rows
            ]


def select_kernel(n_exp, cap, chunks, row_ref, *refs):
    blocks, (weight_ref, keep_ref, send_ref) = refs[:-3], refs[-3:]
    steps, slots = row_ref.shape[:2]
    tok, wide = blocks[0].shape
    picked = [[] for _ in range(chunks)]
    for step in range(steps):
        pick = row_ref[step] == lax.broadcasted_iota(jnp.int32, (slots, 2 * tok), 1)
        pick = pick.astype(F32).astype(BF16)
        for chunk in range(chunks):
            rows = [blocks[(step * 2 + y) * chunks + chunk][...] for y in range(2)]
            rows = jnp.dot(pick, jnp.concatenate(rows, axis=0), preferred_element_type=F32)
            picked[chunk].append(rows.astype(BF16))
    total = None
    for chunk in range(chunks):
        part = jnp.dot(
            jnp.concatenate(picked[chunk], axis=0),
            weight_ref[chunk * wide : (chunk + 1) * wide, :],
            preferred_element_type=F32,
        )
        total = part if total is None else total + part
    total = total.astype(BF16)
    for step in range(steps):
        for j in range(n_exp):
            out = send_ref if j % 2 else keep_ref
            at = step * slots + 2 * cap * j
            out[j // 2, 2 * cap * step : 2 * cap * (step + 1), :] = total[at : at + 2 * cap]


def hidden_kernel(cap, order_ref, stream_ref, mine_ref, came_ref, out_ref, total_ref):
    rows = mine_ref[...].astype(F32) + came_ref[...].astype(F32)
    for i in range(rows.shape[0] // cap):
        to = pl.multiple_of(order_ref[i] * cap, cap)
        total_ref[pl.ds(to, cap), :] = rows[i * cap : (i + 1) * cap]
    out_ref[...] = (total_ref[...] + stream_ref[...].astype(F32)).astype(BF16)


def ffn_kernel(n, blocks, order_ref, *refs):
    pieces, refs = refs[:n], refs[n:]
    gain_ref, gate_ref, up_ref, down_ref, out_ref, rows_ref = refs
    cols = pieces[0].shape[1]
    total = 0.0
    for piece in pieces:
        wide = piece[...].astype(F32)
        total = total + jnp.sum(wide * wide, axis=1, keepdims=True)
    inverse = lax.rsqrt(total * (1.0 / (n * cols)) + 1e-06)
    for i, piece in enumerate(pieces):
        at = lanes(order_ref[i], cols) if n > 1 else slice(None)
        rows_ref[:, at] = (piece[...].astype(F32) * inverse * gain_ref[:, at]).astype(BF16)
    step = out_ref.shape[1] // blocks
    spans = [slice(i * step, (i + 1) * step) for i in range(blocks)]
    gate = up = None
    for at in spans:
        rows = rows_ref[:, at]
        g = jnp.dot(rows, gate_ref[0, at, :], preferred_element_type=F32)
        u = jnp.dot(rows, up_ref[0, at, :], preferred_element_type=F32)
        gate = g if gate is None else gate + g
        up = u if up is None else up + u
    activated = (gate / (1.0 + jnp.exp(-gate)) * up).astype(BF16)
    for at in spans:
        out_ref[:, at] = jnp.dot(
            activated, down_ref[0, :, at], preferred_element_type=F32
        ).astype(BF16)


def per_device(
    stream_in,
    queries,
    key_proj,
    values,
    attn_gate,
    decay_rates,
    attn_gain,
    out_weight,
    ffn_gain,
    routing,
    route_weights,
    w_gate,
    w_up,
    w_down,
):
    tok, width = stream_in.shape
    heads = decay_rates.shape[0]
    size = queries.shape[1] // heads
    n_exp, n_ctx = lax.axis_size("exp"), lax.axis_size("ctx")
    own, place = lax.axis_index("exp"), lax.axis_index("ctx")
    groups = n_ctx // 2
    group, pair = place // 2, place % 2
    cap = tok // 16
    own_rows = tok // n_exp
    cols = out_weight.shape[1]
    hidden_units = w_gate.shape[2]
    per_half = heads // (2 * CHUNKS)
    per_chunk = heads // CHUNKS
    wide = per_chunk * size
    swap = [(i, i ^ 1) for i in range(n_ctx)]
    here = jnp.stack([pair, own]).astype(jnp.int32)
    room = 4 * max(1, n_ctx // 8)

    def swapped(value):
        return lax.ppermute(value, "ctx", swap)

    def shifted(value, by):
        to = [(i, (i + 2 * by) % n_ctx) for i in range(n_ctx)]
        return lax.ppermute(value, "ctx", to)

    def in_hbm(value):
        return pltpu.with_memory_space_constraint(value, pltpu.HBM)

    states = pl.pallas_call(
        functools.partial(state_kernel, per_half),
        out_shape=[jax.ShapeDtypeStruct((per_half, size, size), BF16)] * (2 * CHUNKS),
        in_specs=[SMEM, SMEM, HBM, HBM],
        out_specs=[VMEM] * (2 * CHUNKS),
        scratch_shapes=[
            pltpu.VMEM((tok, heads * size), BF16),
            pltpu.VMEM((tok, heads * size), BF16),
            pltpu.SemaphoreType.DMA((2, CHUNKS)),
        ],
        compiler_params=limit(room),
        cost_estimate=takes(1),
        name="shard_state",
    )(here, decay_rates, in_hbm(key_proj), in_hbm(values))

    def near_part(chunk, start):
        return pl.pallas_call(
            functools.partial(near_kernel, chunk, per_chunk),
            out_shape=[
                jax.ShapeDtypeStruct((tok, wide), F32),
                jax.ShapeDtypeStruct((tok, wide), F32),
                jax.ShapeDtypeStruct((tok, wide), BF16),
            ],
            in_specs=[SMEM] + [VMEM] * 5,
            out_specs=[VMEM] * 3,
            compiler_params=limit(room),
            cost_estimate=takes(1),
            name="near_part",
        )(after(decay_rates, start), queries, key_proj, values, attn_gate, attn_gain[None, :])

    routing = after(routing, states[0])
    hit = routing[:, :, None] == jnp.arange(n_exp, dtype=jnp.int32)
    member = jnp.any(hit, axis=1)
    gate_of = jnp.sum(jnp.where(hit, route_weights[:, :, None], 0.0), axis=1)
    position = jnp.arange(tok, dtype=jnp.int32)
    before = (position[:, None] > position[None, :]).astype(BF16)
    rank = jnp.dot(before, member.astype(BF16), preferred_element_type=F32)
    pick = member[:, :, None] & (rank[:, :, None] == jnp.arange(cap, dtype=F32))
    number = jnp.sum(jnp.where(pick, (position + 1).astype(F32)[:, None, None], 0.0), axis=0)
    own_pick = lax.dynamic_index_in_dim(pick, own, 1, keepdims=False)
    own_weight = jnp.sum(
        jnp.where(own_pick, lax.dynamic_index_in_dim(gate_of, own, 1), 0.0), axis=0
    )
    stream_slots = lax.dot_general(
        own_pick.astype(BF16), stream_in, (((0,), (0,)), ((), ())), preferred_element_type=F32
    ).astype(BF16)
    parcel = stream_slots.reshape(cap, n_ctx, cols).transpose(1, 0, 2)
    label = jnp.pad(number.reshape(1, n_exp * cap), ((0, cap - 1), (0, cols - n_exp * cap)))
    label = jnp.broadcast_to(label.astype(BF16)[None], (n_ctx, cap, cols))
    parcel = jnp.concatenate([parcel, label], axis=1)


    mixed, held = [], None
    for chunk in range(CHUNKS):
        keep, send = states[2 * chunk], states[2 * chunk + 1]
        got = swapped(send if held is None else after(send, held))
        first = chunk * per_chunk + pair * per_half
        rate = lax.dynamic_slice_in_dim(decay_rates, first, per_half, 0)[:, None, None]
        span = jnp.exp(-rate * tok)
        lower = jnp.where(pair == 0, keep, got).astype(F32)
        upper = jnp.where(pair == 0, got, keep).astype(F32)
        window = held = (span * lower + upper).astype(BF16)
        prior = jnp.zeros(lower.shape, F32)
        reach = 1
        while reach < groups:
            line = [(i, i + 2 * reach) for i in range(n_ctx - 2 * reach)]
            far = lax.ppermute(window, "ctx", line).astype(F32)
            prior = prior + jnp.exp(-rate * (2 * tok * (reach - 1))) * far
            window = (window.astype(F32) + jnp.exp(-rate * (2 * tok * reach)) * far).astype(BF16)
            reach *= 2
        near, scale, query = near_part(chunk, far)
        second = span * prior + lower
        mine = jnp.where(pair == 0, prior, second).astype(BF16)
        if chunk == 0:
            mine = after(mine, parcel)
        other = swapped(jnp.where(pair == 0, second, prior).astype(BF16))
        mixed.append(
            pl.pallas_call(
                functools.partial(mix_kernel, chunk, per_half, own_rows),
                out_shape=jax.ShapeDtypeStruct((tok, wide), BF16),
                in_specs=[SMEM, SMEM] + [VMEM] * 5,
                out_specs=VMEM,
                compiler_params=limit(room),
                cost_estimate=takes(1),
                name="mix_heads",
            )(here, decay_rates, query, near, scale, mine, other)
        )

    ring = [[m] for m in mixed]
    cross = [[None] * groups for _ in mixed]
    swaps = []
    for step in range(groups):
        for chunk in range(CHUNKS):
            if step + 1 < groups:
                ring[chunk].append(shifted(ring[chunk][step], 1))
        for chunk in range(CHUNKS):
            if chunk % 2 == 0 or step != 1:
                held = swaps[-2:-1] if len(swaps) > 1 else []
                cross[chunk][step] = swapped(after(ring[chunk][step], *held))
                swaps.append(cross[chunk][step])
    for chunk in range(1, CHUNKS, 2):
        cross[chunk][1] = shifted(after(cross[chunk][0], ring[chunk - 1][-1]), 1)
    rows_of = [
        [[r[step] for r in ring], [c[step] for c in cross]] for step in range(groups)
    ]

    arrived = lax.all_to_all(
        after(parcel, ring[0][-1]), "ctx", split_axis=0, concat_axis=0, tiled=True
    )
    stream_rows = arrived[:, :cap].reshape(n_ctx * cap, cols)
    token = arrived[:, cap, : n_exp * cap].astype(jnp.int32).reshape(n_ctx, n_exp, cap) - 1
    index = jnp.arange(n_ctx, dtype=jnp.int32)
    order = ((group - index // 2) % groups) * 2 + (pair ^ (index % 2))
    row = (index % 2 ^ pair)[:, None, None] * n_exp + ((token // own_rows) ^ own)
    row = jnp.where(token >= 0, row * own_rows + token % own_rows, -1)
    row = jnp.stack(
        [lax.dynamic_index_in_dim(row, own ^ j, 1, keepdims=False) for j in range(n_exp)], axis=1
    )
    row = jnp.take(row, order, axis=0).reshape(groups, 2, n_exp, cap)
    row = row.transpose(0, 2, 1, 3).reshape(groups, n_exp * 2 * cap, 1)

    slots = jax.ShapeDtypeStruct((n_exp // 2, n_ctx * cap, cols), BF16)
    slot_parts = pl.pallas_call(
        functools.partial(select_kernel, n_exp, cap, CHUNKS),
        out_shape=[slots, slots],
        in_specs=[VMEM] * (2 + n_ctx * CHUNKS),
        out_specs=[VMEM] * 2,
        compiler_params=limit(room),
        cost_estimate=takes(1),
        name="slot_rows",
    )(
        row,
        *[rows_of[i // 2][i % 2][chunk] for i in range(n_ctx) for chunk in range(CHUNKS)],
        out_weight,
    )

    parts = []
    for step in range(groups):
        weight = out_weight
        weight = after(weight, cross[0][-1] if step + 1 < groups else slot_parts[0])
        rows = jax.ShapeDtypeStruct((n_exp // 2, 2 * own_rows, cols), BF16)
        parts.append(
            pl.pallas_call(
                functools.partial(project_kernel, n_exp),
                out_shape=[rows, rows],
                in_specs=[VMEM] * (1 + 2 * CHUNKS),
                out_specs=[VMEM] * 2,
                compiler_params=limit(room),
                cost_estimate=takes(1.5 if step + 1 < groups else 60),
                name="project",
            )(*[rows_of[step][y][chunk] for chunk in range(CHUNKS) for y in range(2)], weight)
        )
    def add_groups(keep, send):
        came = lax.ppermute(send, "exp", [(i, i ^ 1) for i in range(n_exp)])
        bit = 2
        while bit < n_exp:
            total = (keep.astype(F32) + came.astype(F32)).astype(BF16)
            total = total.reshape(n_exp // (2 * bit), 2, *total.shape[1:])
            keep = total[:, 0]
            came = lax.ppermute(total[:, 1], "exp", [(i, i ^ bit) for i in range(n_exp)])
            bit *= 2
        return keep[0], came[0]

    hidden = pl.pallas_call(
        functools.partial(hidden_kernel, cap),
        out_shape=jax.ShapeDtypeStruct((n_ctx * cap, cols), BF16),
        in_specs=[SMEM] + [VMEM] * 3,
        out_specs=VMEM,
        scratch_shapes=[pltpu.VMEM((n_ctx * cap, cols), F32)],
        compiler_params=limit(room),
        cost_estimate=takes(1),
        name="slot_hidden",
    )(order, stream_rows, *add_groups(*slot_parts))

    pieces = {0: hidden}
    bit = 1
    while bit < groups:
        for r in range(bit):
            pieces[r | bit] = lax.ppermute(
                pieces[r], "ctx", [(i, i ^ (2 * bit)) for i in range(n_ctx)]
            )
        bit *= 2
    pieces = [p for r in range(groups) for p in (pieces[r], swapped(pieces[r]))]
    late = pieces[-3:-1]
    source = (place ^ index).astype(jnp.int32)
    if cols % 128:
        pieces = [jnp.take(jnp.stack(pieces), source, axis=0).transpose(1, 0, 2).reshape(-1, width)]

    bulk_parts = [jnp.concatenate([p[i] for p in parts], axis=1) for i in (0, 1)]
    mine, came = add_groups(bulk_parts[0], after(bulk_parts[1], *late))
    bulk = (mine.astype(F32) + came.astype(F32)).astype(BF16)
    bulk = bulk.reshape(groups, 2, own_rows, cols)

    blocks = 8
    down = pl.pallas_call(
        functools.partial(ffn_kernel, len(pieces), blocks),
        out_shape=jax.ShapeDtypeStruct((n_ctx * cap, width), BF16),
        in_specs=[SMEM] + [VMEM] * (len(pieces) + 4),
        out_specs=VMEM,
        scratch_shapes=[
            pltpu.VMEM((n_ctx * cap, width), BF16),
        ],
        compiler_params=limit(room),
        cost_estimate=takes(10),
        name="expert",
    )(source, *pieces, ffn_gain[None, :], w_gate, w_up, w_down)
    received = lax.all_to_all(
        down.reshape(n_ctx, cap, width), "ctx", split_axis=0, concat_axis=0, tiled=True
    )
    summed = jnp.sum(received.astype(F32), axis=0)
    expert_out = (summed * own_weight[:, None]).astype(BF16).reshape(1, 1, cap, width)

    turned = jnp.stack([bulk[:, 0], swapped(bulk[:, 1])], axis=1)
    back = [turned[0]] + [shifted(turned[k], -k) for k in range(1, groups)]
    order = ((index // 2 - group) % groups) * 2 + (pair ^ (index % 2))
    projected = jnp.take(jnp.concatenate(back), order, axis=0).transpose(1, 0, 2)
    projected = projected.reshape(own_rows, width)
    stream_own = lax.dynamic_slice_in_dim(stream_in, own * own_rows, own_rows, 0)
    residual_out = (stream_own.astype(F32) + projected.astype(F32)).astype(BF16)
    return (residual_out, expert_out)


def solution(mesh):
    return jax.shard_map(
        per_device,
        mesh=mesh,
        in_specs=(
            P("ctx", None),
            P("ctx", "exp"),
            P("ctx", "exp"),
            P("ctx", "exp"),
            P("ctx", "exp"),
            P("exp"),
            P("exp"),
            P("exp", "ctx"),
            P(),
            P("ctx", None),
            P("ctx", None),
            P("exp", None, "ctx"),
            P("exp", None, "ctx"),
            P("exp", "ctx", None),
        ),
        out_specs=(P(("ctx", "exp"), None), P("ctx", "exp", None, None)),
        check_vma=False,
    )
```

```python
import functools

import jax
import jax.numpy as jnp
from jax import lax
from jax.experimental import pallas as pl
from jax.experimental.pallas import tpu as pltpu
from jax.sharding import PartitionSpec as P

CHUNKS = 2
F32 = jnp.float32
BF16 = jnp.bfloat16
VMEM = pl.BlockSpec(memory_space=pltpu.VMEM)
SMEM = pl.BlockSpec(memory_space=pltpu.SMEM)
HBM = pl.BlockSpec(memory_space=pltpu.HBM)


def limit(mib):
    return pltpu.CompilerParams(vmem_limit_bytes=mib * 2**20)


def takes(us):
    return pl.CostEstimate(flops=int(us * 1e9), bytes_accessed=int(1e6), transcendentals=0)


def rows_iota(shape):
    return lax.broadcasted_iota(jnp.int32, shape, 0).astype(F32)


def cols_iota(shape):
    return lax.broadcasted_iota(jnp.int32, shape, 1).astype(F32)


def lanes(head, size):
    return pl.ds(pl.multiple_of(head * size, size), size)


def after(value, *others):
    return lax.optimization_barrier((value, *others))[0]


def state_kernel(per_half, place_ref, decay_ref, k_hbm, v_hbm, *refs):
    outs, (k_ref, v_ref, sems) = refs[: 2 * CHUNKS], refs[2 * CHUNKS :]
    pair = place_ref[0]
    tok, size = k_ref.shape[0], outs[0].shape[2]
    wide = k_ref.shape[1] // CHUNKS
    copies = []
    for chunk in range(CHUNKS):
        at = pl.ds(chunk * wide, wide)
        copies.append(
            [
                pltpu.make_async_copy(hbm.at[:, at], ref.at[:, at], sems.at[i, chunk])
                for i, (hbm, ref) in enumerate(((k_hbm, k_ref), (v_hbm, v_ref)))
            ]
        )
        for copy in copies[-1]:
            copy.start()
    back = (tok - 1.0) - rows_iota((tok, size))
    for chunk in range(CHUNKS):
        for copy in copies[chunk]:
            copy.wait()
        for which in (1, 0):
            half = pair if which == 0 else 1 - pair
            heads = [chunk * 2 * per_half + half * per_half + l for l in range(per_half)]
            keys = [
                (k_ref[:, lanes(h, size)].astype(F32) * jnp.exp(-decay_ref[h] * back)).astype(BF16)
                for h in heads
            ]
            states = [
                lax.dot_general(
                    k,
                    v_ref[:, lanes(h, size)],
                    (((0,), (0,)), ((), ())),
                    preferred_element_type=F32,
                )
                for k, h in zip(keys, heads)
            ]
            for l, state in enumerate(states):
                outs[chunk * 2 + which][l] = state.astype(BF16)


def near_kernel(chunk, heads, decay_ref, q_ref, k_ref, v_ref, gate_ref, gain_ref, near_ref, scale_ref, query_ref):
    tok = q_ref.shape[0]
    size = near_ref.shape[1] // heads
    gap = rows_iota((tok, tok)) - cols_iota((tok, tok))
    ahead = jnp.maximum(gap, 0.0)
    for first in range(0, heads, 4):
        local = range(first, min(first + 4, heads))
        at = [slice((chunk * heads + l) * size, (chunk * heads + l + 1) * size) for l in local]
        scores = [
            lax.dot_general(
                q_ref[:, s], k_ref[:, s], (((1,), (1,)), ((), ())), preferred_element_type=F32
            )
            for s in at
        ]
        weights = []
        for l, score in zip(local, scores):
            mask = jnp.where(gap >= 0.0, jnp.exp(-decay_ref[chunk * heads + l] * ahead), 0.0)
            weights.append((score * mask).astype(BF16))
        for l, s, w in zip(local, at, weights):
            near_ref[:, l * size : (l + 1) * size] = jnp.dot(
                w, v_ref[:, s], preferred_element_type=F32
            )
    own = slice(chunk * heads * size, (chunk + 1) * heads * size)
    gate = gate_ref[:, own].astype(F32)
    scale_ref[...] = gain_ref[:, own] / (1.0 + jnp.exp(-gate))
    query_ref[...] = q_ref[:, own]


def mix_kernel(
    chunk, per_half, own_rows, place_ref, decay_ref, q_ref, near_ref, scale_ref, mine_ref, other_ref, out_ref
):
    pair, own = place_ref[0], place_ref[1]
    size = mine_ref.shape[2]
    tok = q_ref.shape[0]
    ahead = rows_iota((tok, size)) + 1.0
    for which in range(2):
        prior = mine_ref if which == 0 else other_ref
        half = pair if which == 0 else 1 - pair
        local = [half * per_half + l for l in range(per_half)]
        far = [
            jnp.dot(q_ref[:, lanes(h, size)], prior[l], preferred_element_type=F32)
            for l, h in enumerate(local)
        ]
        mixed = []
        for h, part in zip(local, far):
            decay = decay_ref[chunk * 2 * per_half + h]
            attended = near_ref[:, lanes(h, size)] + part * jnp.exp(-decay * ahead)
            inverse = lax.rsqrt(jnp.mean(attended * attended, axis=1, keepdims=True) + 1e-06)
            mixed.append((attended * inverse * scale_ref[:, lanes(h, size)]).astype(BF16))
        for h, rows in zip(local, mixed):
            for block in range(tok // own_rows):
                to = pl.multiple_of((block ^ own) * own_rows, own_rows)
                out_ref[pl.ds(to, own_rows), lanes(h, size)] = rows[
                    block * own_rows : (block + 1) * own_rows
                ]


def project_kernel(n_exp, *refs):
    weight_ref, outs = refs[-3], refs[-2:]
    pairs = refs[:-3]
    chunks = len(pairs) // 2
    wide = pairs[0].shape[1]
    own_rows = pairs[0].shape[0] // n_exp
    for y in range(2):
        total = None
        for chunk in range(chunks):
            part = jnp.dot(
                pairs[chunk * 2 + y][...],
                weight_ref[chunk * wide : (chunk + 1) * wide, :],
                preferred_element_type=F32,
            )
            total = part if total is None else total + part
        rows = total.astype(BF16)
        for j in range(n_exp):
            outs[j % 2][j // 2, y * own_rows : (y + 1) * own_rows, :] = rows[
                j * own_rows : (j + 1) * own_rows
            ]


def select_kernel(n_exp, cap, chunks, row_ref, *refs):
    blocks, (weight_ref, keep_ref, send_ref) = refs[:-3], refs[-3:]
    steps, _, slots = row_ref.shape
    tok, wide = blocks[0].shape
    picked = [[] for _ in range(chunks)]
    for step in range(steps):
        pick = row_ref[step] == lax.broadcasted_iota(jnp.int32, (2 * tok, slots), 0)
        pick = pick.astype(F32).astype(BF16)
        for chunk in range(chunks):
            rows = [blocks[(step * 2 + y) * chunks + chunk][...] for y in range(2)]
            rows = lax.dot_general(
                pick,
                jnp.concatenate(rows, axis=0),
                (((0,), (0,)), ((), ())),
                preferred_element_type=F32,
            )
            picked[chunk].append(rows.astype(BF16))
    total = None
    for chunk in range(chunks):
        part = jnp.dot(
            jnp.concatenate(picked[chunk], axis=0),
            weight_ref[chunk * wide : (chunk + 1) * wide, :],
            preferred_element_type=F32,
        )
        total = part if total is None else total + part
    total = total.astype(BF16)
    for step in range(steps):
        for j in range(n_exp):
            out = send_ref if j % 2 else keep_ref
            at = step * slots + 2 * cap * j
            out[j // 2, 2 * cap * step : 2 * cap * (step + 1), :] = total[at : at + 2 * cap]


def hidden_kernel(cap, order_ref, stream_ref, mine_ref, came_ref, out_ref, total_ref):
    rows = mine_ref[...].astype(F32) + came_ref[...].astype(F32)
    for i in range(rows.shape[0] // cap):
        to = pl.multiple_of(order_ref[i] * cap, cap)
        total_ref[pl.ds(to, cap), :] = rows[i * cap : (i + 1) * cap]
    out_ref[...] = (total_ref[...] + stream_ref[...].astype(F32)).astype(BF16)


def ffn_kernel(n, blocks, order_ref, *refs):
    pieces, refs = refs[:n], refs[n:]
    gain_ref, gate_ref, up_ref, down_ref, out_ref, rows_ref = refs
    cols = pieces[0].shape[1]
    total = 0.0
    for piece in pieces:
        wide = piece[...].astype(F32)
        total = total + jnp.sum(wide * wide, axis=1, keepdims=True)
    inverse = lax.rsqrt(total * (1.0 / (n * cols)) + 1e-06)
    for i, piece in enumerate(pieces):
        at = lanes(order_ref[i], cols) if n > 1 else slice(None)
        rows_ref[:, at] = (piece[...].astype(F32) * inverse * gain_ref[:, at]).astype(BF16)
    step = out_ref.shape[1] // blocks
    spans = [slice(i * step, (i + 1) * step) for i in range(blocks)]
    gate = up = None
    for at in spans:
        rows = rows_ref[:, at]
        g = jnp.dot(rows, gate_ref[0, at, :], preferred_element_type=F32)
        u = jnp.dot(rows, up_ref[0, at, :], preferred_element_type=F32)
        gate = g if gate is None else gate + g
        up = u if up is None else up + u
    activated = (gate / (1.0 + jnp.exp(-gate)) * up).astype(BF16)
    for at in spans:
        out_ref[:, at] = jnp.dot(
            activated, down_ref[0, :, at], preferred_element_type=F32
        ).astype(BF16)


def per_device(
    stream_in,
    queries,
    key_proj,
    values,
    attn_gate,
    decay_rates,
    attn_gain,
    out_weight,
    ffn_gain,
    routing,
    route_weights,
    w_gate,
    w_up,
    w_down,
):
    tok, width = stream_in.shape
    heads = decay_rates.shape[0]
    size = queries.shape[1] // heads
    n_exp, n_ctx = lax.axis_size("exp"), lax.axis_size("ctx")
    own, place = lax.axis_index("exp"), lax.axis_index("ctx")
    groups = n_ctx // 2
    group, pair = place // 2, place % 2
    cap = tok // 16
    own_rows = tok // n_exp
    cols = out_weight.shape[1]
    hidden_units = w_gate.shape[2]
    per_half = heads // (2 * CHUNKS)
    per_chunk = heads // CHUNKS
    wide = per_chunk * size
    swap = [(i, i ^ 1) for i in range(n_ctx)]
    here = jnp.stack([pair, own]).astype(jnp.int32)
    room = 4 * max(1, n_ctx // 8)

    def swapped(value):
        return lax.ppermute(value, "ctx", swap)

    def shifted(value, by):
        to = [(i, (i + 2 * by) % n_ctx) for i in range(n_ctx)]
        return lax.ppermute(value, "ctx", to)

    def in_hbm(value):
        return pltpu.with_memory_space_constraint(value, pltpu.HBM)

    states = pl.pallas_call(
        functools.partial(state_kernel, per_half),
        out_shape=[jax.ShapeDtypeStruct((per_half, size, size), BF16)] * (2 * CHUNKS),
        in_specs=[SMEM, SMEM, HBM, HBM],
        out_specs=[VMEM] * (2 * CHUNKS),
        scratch_shapes=[
            pltpu.VMEM((tok, heads * size), BF16),
            pltpu.VMEM((tok, heads * size), BF16),
            pltpu.SemaphoreType.DMA((2, CHUNKS)),
        ],
        compiler_params=limit(room),
        cost_estimate=takes(1),
        name="shard_state",
    )(here, decay_rates, in_hbm(key_proj), in_hbm(values))

    def near_part(chunk, start):
        return pl.pallas_call(
            functools.partial(near_kernel, chunk, per_chunk),
            out_shape=[
                jax.ShapeDtypeStruct((tok, wide), F32),
                jax.ShapeDtypeStruct((tok, wide), F32),
                jax.ShapeDtypeStruct((tok, wide), BF16),
            ],
            in_specs=[SMEM] + [VMEM] * 5,
            out_specs=[VMEM] * 3,
            compiler_params=limit(room),
            cost_estimate=takes(1),
            name="near_part",
        )(after(decay_rates, start), queries, key_proj, values, attn_gate, attn_gain[None, :])

    routing = after(routing, states[0])
    hit = routing[:, :, None] == jnp.arange(n_exp, dtype=jnp.int32)
    member = jnp.any(hit, axis=1)
    gate_of = jnp.sum(jnp.where(hit, route_weights[:, :, None], 0.0), axis=1)
    position = jnp.arange(tok, dtype=jnp.int32)
    before = (position[:, None] > position[None, :]).astype(BF16)
    rank = jnp.dot(before, member.astype(BF16), preferred_element_type=F32)
    pick = member[:, :, None] & (rank[:, :, None] == jnp.arange(cap, dtype=F32))
    number = jnp.sum(jnp.where(pick, (position + 1).astype(F32)[:, None, None], 0.0), axis=0)
    own_pick = lax.dynamic_index_in_dim(pick, own, 1, keepdims=False)
    own_weight = jnp.sum(
        jnp.where(own_pick, lax.dynamic_index_in_dim(gate_of, own, 1), 0.0), axis=0
    )
    stream_slots = lax.dot_general(
        own_pick.astype(BF16), stream_in, (((0,), (0,)), ((), ())), preferred_element_type=F32
    ).astype(BF16)
    parcel = stream_slots.reshape(cap, n_ctx, cols).transpose(1, 0, 2)
    label = jnp.pad(number.reshape(1, n_exp * cap), ((0, cap - 1), (0, cols - n_exp * cap)))
    label = jnp.broadcast_to(label.astype(BF16)[None], (n_ctx, cap, cols))
    parcel = jnp.concatenate([parcel, label], axis=1)


    mixed, held = [], None
    for chunk in range(CHUNKS):
        keep, send = states[2 * chunk], states[2 * chunk + 1]
        got = swapped(send if held is None else after(send, held))
        first = chunk * per_chunk + pair * per_half
        rate = lax.dynamic_slice_in_dim(decay_rates, first, per_half, 0)[:, None, None]
        span = jnp.exp(-rate * tok)
        lower = jnp.where(pair == 0, keep, got).astype(F32)
        upper = jnp.where(pair == 0, got, keep).astype(F32)
        window = held = (span * lower + upper).astype(BF16)
        prior = jnp.zeros(lower.shape, F32)
        reach = 1
        while reach < groups:
            line = [(i, i + 2 * reach) for i in range(n_ctx - 2 * reach)]
            far = lax.ppermute(window, "ctx", line).astype(F32)
            prior = prior + jnp.exp(-rate * (2 * tok * (reach - 1))) * far
            window = (window.astype(F32) + jnp.exp(-rate * (2 * tok * reach)) * far).astype(BF16)
            reach *= 2
        near, scale, query = near_part(chunk, far)
        second = span * prior + lower
        mine = jnp.where(pair == 0, prior, second).astype(BF16)
        if chunk == 0:
            mine = after(mine, parcel)
        other = swapped(jnp.where(pair == 0, second, prior).astype(BF16))
        mixed.append(
            pl.pallas_call(
                functools.partial(mix_kernel, chunk, per_half, own_rows),
                out_shape=jax.ShapeDtypeStruct((tok, wide), BF16),
                in_specs=[SMEM, SMEM] + [VMEM] * 5,
                out_specs=VMEM,
                compiler_params=limit(room),
                cost_estimate=takes(1),
                name="mix_heads",
            )(here, decay_rates, query, near, scale, mine, other)
        )

    ring = [[m] for m in mixed]
    cross = [[None] * groups for _ in mixed]
    swaps = []
    for step in range(groups):
        for chunk in range(CHUNKS):
            if step + 1 < groups:
                ring[chunk].append(shifted(ring[chunk][step], 1))
        for chunk in range(CHUNKS):
            if chunk % 2 == 0 or step != 1:
                held = swaps[-2:-1] if len(swaps) > 1 else []
                cross[chunk][step] = swapped(after(ring[chunk][step], *held))
                swaps.append(cross[chunk][step])
    for chunk in range(1, CHUNKS, 2):
        cross[chunk][1] = shifted(after(cross[chunk][0], ring[chunk - 1][-1]), 1)
    rows_of = [
        [[r[step] for r in ring], [c[step] for c in cross]] for step in range(groups)
    ]

    arrived = lax.all_to_all(
        after(parcel, ring[0][-1]), "ctx", split_axis=0, concat_axis=0, tiled=True
    )
    stream_rows = arrived[:, :cap].reshape(n_ctx * cap, cols)
    token = arrived[:, cap, : n_exp * cap].astype(jnp.int32).reshape(n_ctx, n_exp, cap) - 1
    index = jnp.arange(n_ctx, dtype=jnp.int32)
    order = ((group - index // 2) % groups) * 2 + (pair ^ (index % 2))
    row = (index % 2 ^ pair)[:, None, None] * n_exp + ((token // own_rows) ^ own)
    row = jnp.where(token >= 0, row * own_rows + token % own_rows, -1)
    row = jnp.stack(
        [lax.dynamic_index_in_dim(row, own ^ j, 1, keepdims=False) for j in range(n_exp)], axis=1
    )
    row = jnp.take(row, order, axis=0).reshape(groups, 2, n_exp, cap)
    row = row.transpose(0, 2, 1, 3).reshape(groups, 1, n_exp * 2 * cap)

    slots = jax.ShapeDtypeStruct((n_exp // 2, n_ctx * cap, cols), BF16)
    slot_parts = pl.pallas_call(
        functools.partial(select_kernel, n_exp, cap, CHUNKS),
        out_shape=[slots, slots],
        in_specs=[VMEM] * (2 + n_ctx * CHUNKS),
        out_specs=[VMEM] * 2,
        compiler_params=limit(room),
        cost_estimate=takes(1),
        name="slot_rows",
    )(
        row,
        *[rows_of[i // 2][i % 2][chunk] for i in range(n_ctx) for chunk in range(CHUNKS)],
        out_weight,
    )

    parts = []
    for step in range(groups):
        weight = out_weight
        weight = after(weight, cross[0][-1] if step + 1 < groups else slot_parts[0])
        rows = jax.ShapeDtypeStruct((n_exp // 2, 2 * own_rows, cols), BF16)
        parts.append(
            pl.pallas_call(
                functools.partial(project_kernel, n_exp),
                out_shape=[rows, rows],
                in_specs=[VMEM] * (1 + 2 * CHUNKS),
                out_specs=[VMEM] * 2,
                compiler_params=limit(room),
                cost_estimate=takes(1.5 if step + 1 < groups else 60),
                name="project",
            )(*[rows_of[step][y][chunk] for chunk in range(CHUNKS) for y in range(2)], weight)
        )
    def add_groups(keep, send):
        came = lax.ppermute(send, "exp", [(i, i ^ 1) for i in range(n_exp)])
        bit = 2
        while bit < n_exp:
            total = (keep.astype(F32) + came.astype(F32)).astype(BF16)
            total = total.reshape(n_exp // (2 * bit), 2, *total.shape[1:])
            keep = total[:, 0]
            came = lax.ppermute(total[:, 1], "exp", [(i, i ^ bit) for i in range(n_exp)])
            bit *= 2
        return keep[0], came[0]

    hidden = pl.pallas_call(
        functools.partial(hidden_kernel, cap),
        out_shape=jax.ShapeDtypeStruct((n_ctx * cap, cols), BF16),
        in_specs=[SMEM] + [VMEM] * 3,
        out_specs=VMEM,
        scratch_shapes=[pltpu.VMEM((n_ctx * cap, cols), F32)],
        compiler_params=limit(room),
        cost_estimate=takes(1),
        name="slot_hidden",
    )(order, stream_rows, *add_groups(*slot_parts))

    pieces = {0: hidden}
    bit = 1
    while bit < groups:
        for r in range(bit):
            pieces[r | bit] = lax.ppermute(
                pieces[r], "ctx", [(i, i ^ (2 * bit)) for i in range(n_ctx)]
            )
        bit *= 2
    pieces = [p for r in range(groups) for p in (pieces[r], swapped(pieces[r]))]
    late = pieces[-3:-1]
    source = (place ^ index).astype(jnp.int32)
    if cols % 128:
        pieces = [jnp.take(jnp.stack(pieces), source, axis=0).transpose(1, 0, 2).reshape(-1, width)]

    bulk_parts = [jnp.concatenate([p[i] for p in parts], axis=1) for i in (0, 1)]
    mine, came = add_groups(bulk_parts[0], after(bulk_parts[1], *late))
    bulk = (mine.astype(F32) + came.astype(F32)).astype(BF16)
    bulk = bulk.reshape(groups, 2, own_rows, cols)

    blocks = 8
    down = pl.pallas_call(
        functools.partial(ffn_kernel, len(pieces), blocks),
        out_shape=jax.ShapeDtypeStruct((n_ctx * cap, width), BF16),
        in_specs=[SMEM] + [VMEM] * (len(pieces) + 4),
        out_specs=VMEM,
        scratch_shapes=[
            pltpu.VMEM((n_ctx * cap, width), BF16),
        ],
        compiler_params=limit(room),
        cost_estimate=takes(10),
        name="expert",
    )(source, *pieces, ffn_gain[None, :], w_gate, w_up, w_down)
    received = lax.all_to_all(
        down.reshape(n_ctx, cap, width), "ctx", split_axis=0, concat_axis=0, tiled=True
    )
    summed = jnp.sum(received.astype(F32), axis=0)
    expert_out = (summed * own_weight[:, None]).astype(BF16).reshape(1, 1, cap, width)

    turned = jnp.stack([bulk[:, 0], swapped(bulk[:, 1])], axis=1)
    back = [turned[0]] + [shifted(turned[k], -k) for k in range(1, groups)]
    order = ((index // 2 - group) % groups) * 2 + (pair ^ (index % 2))
    projected = jnp.take(jnp.concatenate(back), order, axis=0).transpose(1, 0, 2)
    projected = projected.reshape(own_rows, width)
    stream_own = lax.dynamic_slice_in_dim(stream_in, own * own_rows, own_rows, 0)
    residual_out = (stream_own.astype(F32) + projected.astype(F32)).astype(BF16)
    return (residual_out, expert_out)


def solution(mesh):
    return jax.shard_map(
        per_device,
        mesh=mesh,
        in_specs=(
            P("ctx", None),
            P("ctx", "exp"),
            P("ctx", "exp"),
            P("ctx", "exp"),
            P("ctx", "exp"),
            P("exp"),
            P("exp"),
            P("exp", "ctx"),
            P(),
            P("ctx", None),
            P("ctx", None),
            P("exp", None, "ctx"),
            P("exp", None, "ctx"),
            P("exp", "ctx", None),
        ),
        out_specs=(P(("ctx", "exp"), None), P("ctx", "exp", None, None)),
        check_vma=False,
    )
```
